512 devices in a mesh: leaf: 512 (over x, z, y, core).
Axes of the slice: x: 4, y: 8, z: 8, core: 2. Of those that a mesh axis runs over, the one named last changes fastest.
Arguments:
- values: bfloat16 [1572864, 128], P('leaf'), may hold values from -6 to 6
- points: float32 [8, 1572864], P(None, 'leaf'), may hold values from -6 to 6
- tree_order: int32 [512, 3072], P('leaf'), may hold values from 0 to 3071, each once within a row
- leaf_sizes: int32 [512, 16], P('leaf'), may hold values from 1 to 256, 3072 in all within a row
- leaf_basis: bfloat16 [8192, 256, 128], P('leaf'), may hold values from -0.375 to 0.375
- local_transfer: bfloat16 [7680, 2, 128, 128], P('leaf'), may hold values from -0.4375 to 0.4375
- local_coupling: bfloat16 [7680, 128, 128], P('leaf'), may hold values from -0.5 to 0.5
- cross_transfer: bfloat16 [512, 2, 128, 128], P('leaf'), may hold values from -0.4375 to 0.4375
- cross_coupling: bfloat16 [512, 128, 128], P('leaf'), may hold values from -0.5 to 0.5
Outputs:
- product_values: bfloat16 [1572864, 128], P('leaf')
The draws below stay inside these ranges and needn't reach their ends.
Inputs may be any that keep to these rules, and one draw needn't show every extreme that they name: `tree_order`: each row is a permutation of 0 .. 3071. `leaf_sizes`: each row sums to 3072; its largest entry is 256.
All inputs are finite; a program needn't handle non-finite values.
Results may differ from the reference program's by a relative error of at most 0.0048.
Values sent between devices are 32-bit elements; how exact they have to be, the bound alone decides.
A program may use at most 64 MiB of HBM per device.

```python
import math
import jax
import jax.numpy as jnp
import numpy as np
from jax import lax

DIM = 8
LEAF = 256
RANK = 128
RHS = 128
LEAVES_DEV = 16
PTS_DEV = 3072
TOTAL_PTS = 1572864
TOTAL_LEAVES = 8192
N_LEAF = 512


def steps_of(rng, dims, split, low, top_value):
    loudness, own = 1.0, jax.random.fold_in(rng, 6)
    for axis_at, parts in split:
        draws = jnp.exp(jax.random.uniform(jax.random.fold_in(own, axis_at), (parts,), jnp.float32, low / len(split), top_value / len(split)))
        loudness = loudness * jnp.repeat(draws, dims[axis_at] // parts).reshape([-1 if axis == axis_at else 1 for axis in range(len(dims))])
    return loudness


def profile(count, total, limit, lean):
    portions = [(1 << 20) // math.isqrt(grade ** lean) + 1 for grade in range(2, count + 1)]
    surplus, counts = total - limit - (count - 1), [1] * (count - 1)
    while surplus > 0:
        candidates = [i for i in range(count - 1) if counts[i] < limit]
        whole, left = sum([portions[i] for i in candidates]), surplus
        for i in candidates:
            more = min(limit - counts[i], max(1, left * portions[i] // whole), surplus)
            counts[i] = counts[i] + more
            surplus = surplus - more
    return np.array([limit] + counts)


def uneven(stream_key, count, total, most, skew):
    if count == 2:
        one = jax.random.randint(stream_key, (), max(1, total - most), min(most, total - 1) + 1)
        return jnp.stack([one, total - one])
    lengths = jnp.asarray(profile(count, total, most, skew), jnp.int32)
    pairs = (count - 1) // 2
    source_of, taker = lengths[1:1 + 2 * pairs:2], lengths[2:2 + 2 * pairs:2]
    slack = jnp.minimum(source_of - 1, most - taker)
    moved = jax.random.randint(jax.random.fold_in(stream_key, 1), (pairs,), 0, 1 << 20) % (slack + 1)
    lengths = lengths.at[1:1 + 2 * pairs:2].set(source_of - moved).at[2:2 + 2 * pairs:2].set(taker + moved)
    return lengths[jax.random.permutation(jax.random.fold_in(stream_key, 2), count)]


def bell_draw(rng, extent, scale, most, shards=(), kind=jnp.bfloat16):
    array = jax.random.normal(rng, extent, jnp.float32) * scale
    if len(shards) > 0:
        array = steps_of(rng, extent, shards, -0.22, 0.18) * array
    return jnp.clip(array, min=-most, max=most).astype(kind)


def setup_inputs(seed: int = 0) -> dict:
    seeds = jax.random.split(jax.random.key(seed), 10)
    return {
        "values": bell_draw(seeds[0], (TOTAL_PTS, RHS), 1.0, 6.0, ((0, 512),)),
        "points": bell_draw(seeds[1], (DIM, TOTAL_PTS), 1.0, 6.0, ((1, 512),), jnp.float32),
        "tree_order": jax.vmap(lambda own: jax.random.permutation(own, PTS_DEV))(jax.random.split(seeds[2], N_LEAF)).reshape((N_LEAF, PTS_DEV)).astype(jnp.int32),
        "leaf_sizes": jax.vmap(lambda own: uneven(own, LEAVES_DEV, PTS_DEV, LEAF, 0))(jax.random.split(seeds[3], N_LEAF)).reshape((N_LEAF, LEAVES_DEV)).astype(jnp.int32),
        "leaf_basis": bell_draw(seeds[4], (TOTAL_LEAVES, LEAF, RANK), LEAF ** -0.5, 0.375, ((0, 512),)),
        "local_transfer": bell_draw(seeds[5], (N_LEAF * (LEAVES_DEV - 1), 2, RANK, RANK), (3 * RANK // 2) ** -0.5, 0.4375, ((0, 512),)),
        "local_coupling": bell_draw(seeds[6], (N_LEAF * (LEAVES_DEV - 1), RANK, RANK), RANK ** -0.5, 0.5, ((0, 512),)),
        "cross_transfer": bell_draw(seeds[7], (N_LEAF, 2, RANK, RANK), (3 * RANK // 2) ** -0.5, 0.4375, ((0, 512),)),
        "cross_coupling": bell_draw(seeds[8], (N_LEAF, RANK, RANK), RANK ** -0.5, 0.5, ((0, 512),)),
    }


kernel_scale = 8.0
ridge_shift = 1.0
exact_products = lax.Precision.HIGHEST


def arrange(values, points, tree_order, leaf_sizes):
    sizes_int = leaf_sizes.astype(jnp.int32)
    starts = (jnp.cumsum(sizes_int) - sizes_int).astype(jnp.int32)
    within = jnp.arange(LEAF, dtype=jnp.int32)
    position = starts[:, None] + within[None, :]
    inside = within[None, :] < sizes_int[:, None]
    source = tree_order[jnp.clip(position, 0, PTS_DEV - 1)].astype(jnp.int32)
    leaf_rows = jnp.where(inside[:, :, None], values[source], jnp.zeros((), values.dtype))
    leaf_points = points[:, source]
    target = jnp.where(inside, source, PTS_DEV).astype(jnp.int32)
    return leaf_rows, leaf_points, target


def leaf_kernel(leaf_points):
    squares = jnp.sum(leaf_points * leaf_points, axis=0)
    inner = jnp.einsum('dta,dtb->tab', leaf_points, leaf_points, precision=exact_products)
    distance = squares[:, :, None] + squares[:, None, :] - 2.0 * inner
    unit = jnp.eye(LEAF, dtype=jnp.float32)
    return (jnp.exp(-distance / kernel_scale) + ridge_shift * unit).astype(jnp.bfloat16)


def climb(coefficients, transfer, coupling):
    transfer = transfer.astype(jnp.float32)
    coupling = coupling.astype(jnp.float32)
    left_part = coefficients[0::2]
    right_part = coefficients[1::2]
    parent = jnp.einsum('jkq,jkr->jqr', transfer[:, 0], left_part, precision=exact_products)
    parent = parent + jnp.einsum('jkq,jkr->jqr', transfer[:, 1], right_part, precision=exact_products)
    toward_left = jnp.einsum('jqk,jkr->jqr', coupling, right_part, precision=exact_products)
    toward_right = jnp.einsum('jkq,jkr->jqr', coupling, left_part, precision=exact_products)
    return parent, toward_left, toward_right


def descend(field, toward_left, toward_right, transfer):
    transfer = transfer.astype(jnp.float32)
    left_field = toward_left + jnp.einsum('jqk,jkr->jqr', transfer[:, 0], field, precision=exact_products)
    right_field = toward_right + jnp.einsum('jqk,jkr->jqr', transfer[:, 1], field, precision=exact_products)
    return jnp.stack([left_field, right_field], 1).reshape((-1,) + field.shape[1:])


def local_up(leaf_rows, basis, transfer, coupling):
    coefficients = jnp.einsum('tak,tar->tkr', basis.astype(jnp.float32), leaf_rows.astype(jnp.float32), precision=exact_products)
    stored = []
    offset = 0
    nodes = LEAVES_DEV
    for section in range(LEAVES_DEV.bit_length() - 1):
        half = nodes // 2
        coefficients, toward_left, toward_right = climb(coefficients, transfer[offset:offset + half], coupling[offset:offset + half])
        stored.append((toward_left, toward_right, offset, half))
        offset = offset + half
        nodes = half
    return coefficients, stored


def reference(values, points, tree_order, leaf_sizes, leaf_basis, local_transfer, local_coupling, cross_transfer, cross_coupling):
    per_values = values.reshape(N_LEAF, PTS_DEV, RHS)
    per_points = jnp.transpose(points.reshape(DIM, N_LEAF, PTS_DEV), (1, 0, 2))
    per_basis = leaf_basis.reshape(N_LEAF, LEAVES_DEV, LEAF, RANK)
    per_transfer = local_transfer.reshape(N_LEAF, LEAVES_DEV - 1, 2, RANK, RANK)
    per_coupling = local_coupling.reshape(N_LEAF, LEAVES_DEV - 1, RANK, RANK)

    def device_root(items):
        dev_values, dev_points, dev_order, dev_sizes, dev_basis, dev_transfer, dev_coupling = items
        leaf_rows, leaf_points, target = arrange(dev_values, dev_points, dev_order, dev_sizes)
        root, stored = local_up(leaf_rows, dev_basis, dev_transfer, dev_coupling)
        return root[0]

    roots = lax.map(device_root, (per_values, per_points, tree_order, leaf_sizes, per_basis, per_transfer, per_coupling))

    levels = N_LEAF.bit_length() - 1
    coefficients = roots
    stored_cross = []
    for height in range(1, levels + 1):
        chosen = cross_transfer[2 ** (height - 1)::2 ** height]
        joined = cross_coupling[2 ** (height - 1)::2 ** height]
        coefficients, toward_left, toward_right = climb(coefficients, chosen, joined)
        stored_cross.append((toward_left, toward_right, chosen))
    field = jnp.zeros((1, RANK, RHS), jnp.float32)
    for toward_left, toward_right, chosen in reversed(stored_cross):
        field = descend(field, toward_left, toward_right, chosen)

    def device_output(items):
        dev_values, dev_points, dev_order, dev_sizes, dev_basis, dev_transfer, dev_coupling, dev_field = items
        leaf_rows, leaf_points, target = arrange(dev_values, dev_points, dev_order, dev_sizes)
        root, stored = local_up(leaf_rows, dev_basis, dev_transfer, dev_coupling)
        local_field = dev_field[None]
        for toward_left, toward_right, offset, half in reversed(stored):
            local_field = descend(local_field, toward_left, toward_right, dev_transfer[offset:offset + half])
        kernel = leaf_kernel(leaf_points)
        nearby = jnp.einsum('tab,tbr->tar', kernel.astype(jnp.float32), leaf_rows.astype(jnp.float32), precision=exact_products)
        rounded = local_field.astype(jnp.bfloat16).astype(jnp.float32)
        distant = jnp.einsum('tak,tkr->tar', dev_basis.astype(jnp.float32), rounded, precision=exact_products)
        total = nearby + distant
        result = jnp.zeros((PTS_DEV, RHS), jnp.float32).at[target.reshape(-1)].set(total.reshape(-1, RHS), mode="drop")
        return result.astype(jnp.bfloat16)

    outputs = lax.map(device_output, (per_values, per_points, tree_order, leaf_sizes, per_basis, per_transfer, per_coupling, field))
    return outputs.reshape(TOTAL_PTS, RHS)
```

```python
import functools

import jax
import jax.numpy as jnp
from jax import lax
from jax.experimental import pallas as pl
from jax.experimental.pallas import tpu as pltpu
from jax.sharding import PartitionSpec as P

F32 = jnp.float32
BF16 = jnp.bfloat16
MESH = pl.DeviceIdType.MESH
VMEM = pl.BlockSpec(memory_space=pltpu.VMEM)
SMEM = pl.BlockSpec(memory_space=pltpu.SMEM)
VMEM_LIMIT = 56 * 2**20

PTS = 3072
LEAF = 256
LEAVES = 16
R = 128
UNROLL = 32


def point_pieces(p):
    h = p.astype(BF16).astype(F32)
    rest = p - h
    m = rest.astype(BF16).astype(F32)
    low = (rest - m).astype(BF16).astype(F32)
    q = jnp.sum(p * p, axis=0, keepdims=True) * -0.125
    qh = q.astype(BF16).astype(F32)
    rest = q - qh
    qm = rest.astype(BF16).astype(F32)
    ql = (rest - qm).astype(BF16).astype(F32)
    n = p.shape[1]
    row = lax.broadcasted_iota(jnp.int32, (8, n), 0)
    parts = jnp.where(row % 3 == 0, qh, jnp.where(row % 3 == 1, qm, ql))
    left_q = jnp.where(row < 3, parts, jnp.where(row < 6, 1.0, 0.0))
    right_q = jnp.where(row < 3, 1.0, jnp.where(row < 6, parts, 0.0))
    zero = jnp.zeros((8, n), F32)
    left = [h * 0.25, h * 0.25, m * 0.25, m * 0.25, h * 0.25, low * 0.25, left_q, zero]
    right = [h, m, h, m, low, h, right_q, zero]
    return jnp.concatenate(left + right, axis=0)


def gather_kernel(order, sizes, v_ref, p_ref, rows_out, pts_out, tv, tp, gv, gp):
    tv[...] = v_ref[...].astype(F32)
    for c in range(PTS // 128):
        span = slice(128 * c, 128 * (c + 1))
        tp[span, :] = point_pieces(p_ref[:, span]).T
    gv[PTS:, :] = jnp.zeros((LEAF, R), F32)
    gp[PTS:, :] = jnp.zeros((LEAF, R), F32)

    def move(i, carry):
        base = pl.multiple_of(i * UNROLL, UNROLL)
        for u in range(UNROLL):
            source = order[0, base + u]
            gv[pl.ds(base + u, 1), :] = tv[pl.ds(source, 1), :]
            gp[pl.ds(base + u, 1), :] = tp[pl.ds(source, 1), :]
        return carry

    lax.fori_loop(0, PTS // UNROLL, move, 0)
    slot = lax.broadcasted_iota(jnp.int32, (LEAF, R), 0)
    start = 0
    for t in range(LEAVES):
        size = sizes[0, t]
        rows = gv[pl.ds(start, LEAF), :]
        rows_out[t] = jnp.where(slot < size, rows, 0.0).astype(BF16)
        pts_out[t] = gp[pl.ds(start, LEAF), :].astype(BF16)
        start = start + size


def gather(values, points, order, sizes):
    return pl.pallas_call(
        gather_kernel,
        out_shape=[
            jax.ShapeDtypeStruct((LEAVES, LEAF, R), BF16),
            jax.ShapeDtypeStruct((LEAVES, LEAF, R), BF16),
        ],
        in_specs=[SMEM, SMEM, VMEM, VMEM],
        out_specs=[VMEM, VMEM],
        scratch_shapes=[
            pltpu.VMEM((PTS, R), F32),
            pltpu.VMEM((PTS, R), F32),
            pltpu.VMEM((PTS + LEAF, R), F32),
            pltpu.VMEM((PTS + LEAF, R), F32),
        ],
        compiler_params=pltpu.CompilerParams(vmem_limit_bytes=VMEM_LIMIT),
        name="gather_rows",
    )(order, sizes, values, points)


def scatter_kernel(order, sizes, total, out, tree, held):
    start = 0
    for t in range(LEAVES):
        tree[pl.ds(start, LEAF), :] = total[t].astype(F32)
        start = start + sizes[0, t]

    def move(i, carry):
        base = pl.multiple_of(i * UNROLL, UNROLL)
        for u in range(UNROLL):
            held[pl.ds(order[0, base + u], 1), :] = tree[pl.ds(base + u, 1), :]
        return carry

    lax.fori_loop(0, PTS // UNROLL, move, 0)
    out[...] = held[...].astype(BF16)


def scatter(total, order, sizes):
    return pl.pallas_call(
        scatter_kernel,
        out_shape=jax.ShapeDtypeStruct((PTS, R), BF16),
        in_specs=[SMEM, SMEM, VMEM],
        out_specs=VMEM,
        scratch_shapes=[
            pltpu.VMEM((PTS + LEAF, R), F32),
            pltpu.VMEM((PTS, R), F32),
        ],
        compiler_params=pltpu.CompilerParams(vmem_limit_bytes=VMEM_LIMIT),
        name="scatter_rows",
    )(order, sizes, total)


def dot(a, b, ca=1, cb=0):
    return lax.dot_general(a, b, (((ca,), (cb,)), ((), ())), preferred_element_type=F32)


def split(x):
    h = x.astype(BF16)
    return jnp.concatenate([h, (x - h.astype(F32)).astype(BF16)], axis=0)


def mm(x, w):
    y = dot(split(x), w)
    return y[: x.shape[0]] + y[x.shape[0] :]


def mmt(x, w):
    y = dot(split(x), w, 1, 1)
    return y[: x.shape[0]] + y[x.shape[0] :]


def flip(v, m):
    out = v
    for i in range(3):
        if (m >> i) & 1:
            bit = lax.rem(lax.div(v, 2**i), 2)
            out = out + (1 - 2 * bit) * 2**i
    return out


def reach(m):
    return m.bit_length() - 1


def tree_kernel(
    rows, pts, basis, transfer, coupling, ctrans, ccoup, total,
    coef, term, field, near, own, core_mats, core_coef, up_field,
    path, piece, xpiece, zlev, xlev, mat_w, mat_c,
    prod, yslice, yblock, zsend, zgot, xsend, xgot, gdown, fdown,
    s_core, r_core, s_dir, r_dir, s_m1, r_m1, s_m2, r_m2, s_m3, r_m3, s_m4, r_m4, s_m5, r_m5,
    s_ys, r_ys, s_yb, r_yb, s_z, r_z, s_x, r_x, s_yd, r_yd,
):
    me = lax.axis_index("leaf")
    core = lax.rem(me, 2)
    y = lax.rem(lax.div(me, 2), 8)
    z = lax.rem(lax.div(me, 16), 8)
    x = lax.div(me, 128)
    is0 = core == 0
    is1 = core == 1

    def at(xx, zz, yy):
        return ((xx * 8 + zz) * 8 + yy) * 2

    mate = me + 1 - 2 * core
    along_y = [at(x, z, flip(y, m)) for m in range(8)]
    along_z = [at(x, flip(z, m), y) for m in range(8)]
    along_x = [at(flip(x, m), z, y) for m in range(4)]

    def copy(src, dst, send, recv, to):
        return pltpu.make_async_remote_copy(
            src_ref=src, dst_ref=dst, send_sem=send, recv_sem=recv, device_id=(to,), device_id_type=MESH
        )

    own[0] = ctrans[0, 0].astype(F32)
    own[1] = ccoup[0].astype(F32)
    own[2] = ctrans[0, 1].astype(F32)

    barrier = pltpu.get_barrier_semaphore()
    pl.semaphore_signal(barrier, inc=1, device_id=(mate,), device_id_type=MESH)

    @pl.when(is0)
    def _():
        for to in along_y[1:] + along_z[1:] + along_x[1:]:
            pl.semaphore_signal(barrier, inc=1, device_id=(to,), device_id_type=MESH)
        pl.semaphore_wait(barrier, 18)

    @pl.when(is1)
    def _():
        pl.semaphore_wait(barrier, 1)

    def c_mats():
        return copy(own, core_mats, s_core.at[0], r_core.at[0], mate)

    def c_coef():
        return copy(coef.at[30], core_coef, s_core.at[1], r_core.at[1], mate)

    def c_field():
        return copy(up_field, up_field, s_core.at[2], r_core.at[2], mate)


    def direct(level, i):
        size = 2 << level
        half = size // 2
        src = own.at[0:2] if i < half else own.at[1:3]
        return copy(src, path.at[level], s_dir.at[i], r_dir.at[level], at(x, z, y - half + i))

    def direct_all(level):
        size = 2 << level
        return [direct(level, i) for i in range(size) if i != size // 2]

    def m1(k):
        return copy(own.at[:, 16 * k : 16 * k + 16, :], piece.at[z], s_m1.at[k], r_m1, at(x, z, k))

    def m2(m):
        return copy(piece.at[z], piece.at[z], s_m2.at[m], r_m2.at[m], along_z[m])

    def m2_from(m):
        there = piece.at[flip(z, m)]
        return copy(there, there, s_m2.at[m], r_m2.at[m], along_z[m])

    def m3(m):
        return copy(piece.at[0], xpiece.at[x], s_m3.at[m], r_m3.at[m], along_x[m])

    def m3_from(m):
        return copy(piece.at[0], xpiece.at[flip(x, m)], s_m3.at[m], r_m3.at[m], along_x[m])

    def m4(m):
        return copy(zlev.at[y], zlev.at[y], s_m4.at[m], r_m4.at[m], along_y[m])

    def m4_from(m):
        return copy(zlev.at[y], zlev.at[flip(y, m)], s_m4.at[m], r_m4.at[m], along_y[m])

    def m5(m):
        return copy(xlev.at[y], xlev.at[y], s_m5.at[m], r_m5.at[m], along_y[m])

    def m5_from(m):
        return copy(xlev.at[y], xlev.at[flip(y, m)], s_m5.at[m], r_m5.at[m], along_y[m])

    def ys(m):
        part = prod.at[3, pl.ds(pl.multiple_of(16 * flip(y, m), 16), 16), :]
        return copy(part, yslice.at[m], s_ys.at[m], r_ys.at[m], along_y[m])

    def yb(m):
        return copy(prod.at[reach(m)], yblock.at[m], s_yb.at[m], r_yb.at[m], along_y[m])

    def zs(m):
        return copy(zsend.at[reach(m)], zgot.at[m], s_z.at[m], r_z.at[m], along_z[m])

    def xs(m):
        return copy(xsend.at[reach(m)], xgot.at[m], s_x.at[m], r_x.at[m], along_x[m])

    def yd(m):
        return copy(gdown, fdown.at[y], s_yd.at[m], r_yd.at[m], along_y[m])

    def yd_from(m):
        return copy(gdown, fdown.at[flip(y, m)], s_yd.at[m], r_yd.at[m], along_y[m])

    @pl.when(is1)
    def _():
        c_mats().start()
        core_mats[...] = own[...]

    @pl.when(is0)
    def _():
        @pl.when(y == 0)
        def _():
            for k in range(1, 8):
                m1(k).start()
            piece[z] = own[:, 0:16, :]

        for level in range(3):
            size = 2 << level

            @pl.when(lax.rem(y, size) == size // 2)
            def _():
                for c in direct_all(level):
                    c.start()
                path[level] = own[1:3]

    def leaf(t, carry):
        coef[t] = dot(rows[t], basis[t], 0, 0)
        return carry

    lax.fori_loop(0, LEAVES, leaf, 0, unroll=4)

    eye = (
        lax.broadcasted_iota(jnp.int32, (LEAF, LEAF), 0) == lax.broadcasted_iota(jnp.int32, (LEAF, LEAF), 1)
    ).astype(F32)
    shift = (
        lax.broadcasted_iota(jnp.int32, (R, R), 0) == lax.broadcasted_iota(jnp.int32, (R, R), 1) + 64
    ).astype(F32).astype(BF16)

    def nearby(t, carry):
        left = pts[t]
        right = dot(left, shift).astype(BF16)
        kernel = (jnp.exp(dot(left, right, 1, 1)) + eye).astype(BF16)
        near[t] = dot(kernel, rows[t])
        return carry

    lax.fori_loop(0, 8, nearby, 0, unroll=2)

    @pl.when(is0)
    def _():
        @pl.when(y > 0)
        def _():
            m1(1).wait_recv()

        for m in range(1, 8):
            m2(m).start()

    def climb(j, carry):
        both = jnp.concatenate([coef[2 * j], coef[2 * j + 1]], axis=1)
        coef[16 + j] = mm(both, transfer[j])
        return carry

    lax.fori_loop(0, 8, climb, 0, unroll=4)
    lax.fori_loop(8, 12, climb, 0, unroll=4)
    lax.fori_loop(12, 14, climb, 0, unroll=2)
    climb(14, 0)
    c_coef().start()

    def terms(j, carry):
        term[2 * j] = mmt(coef[2 * j + 1], coupling[j])
        term[2 * j + 1] = mm(coef[2 * j], coupling[j])
        return carry

    lax.fori_loop(0, 15, terms, 0, unroll=3)
    c_coef().wait()

    @pl.when(is0)
    def _():
        for level in range(3):
            size = 2 << level

            @pl.when(lax.rem(y, size) != size // 2)
            def _():
                copy(own.at[0:2], path.at[level], s_dir.at[0], r_dir.at[level], mate).wait_recv()

            side = lax.rem(lax.div(y, size // 2), 2)
            mat_w[level] = path[level, side].astype(BF16)
            c = path[level, 1 - side]
            mat_c[level] = jnp.where(side == 0, c.T, c).astype(BF16)

        c_mats().wait_recv()
        pair = jnp.concatenate([core_mats[0], core_mats[2]], axis=0).astype(BF16)
        prod[0] = mm(jnp.concatenate([coef[30], core_coef[...]], axis=1), pair)
        for level in range(3):
            prod[level + 1] = mm(prod[level], mat_w[level])
        for m in range(1, 8):
            ys(m).start()
        yslice[0] = prod[3, pl.ds(pl.multiple_of(16 * y, 16), 16), :]

        for m in range(1, 8):
            m2_from(m).wait_recv()
        for m in range(1, 4):
            m3(m).start()
        xpiece[x] = piece[0]
        for i in range(3):
            half = 1 << i
            owner = lax.div(z, 2 * half) * 2 * half + half
            side = lax.rem(lax.div(z, half), 2)
            zlev[y, 2 * i] = piece[owner, 2 * side]
            zlev[y, 2 * i + 1] = piece[owner, 1]
        for m in range(1, 8):
            m4(m).start()
        for m in range(1, 4):
            m3_from(m).wait_recv()
        owner = lax.div(x, 2) * 2 + 1
        xlev[y, 0] = xpiece[owner, 2 * lax.rem(x, 2)]
        xlev[y, 1] = xpiece[owner, 1]
        xlev[y, 2] = xpiece[2, 1]
        for m in range(1, 8):
            m5(m).start()
        for m in range(1, 8):
            yb(m).start()

    lax.fori_loop(8, LEAVES, nearby, 0, unroll=2)

    @pl.when(is0)
    def _():
        for m in range(1, 8):
            m4_from(m).wait_recv()
        for i in range(3):
            mat_w[3 + i] = zlev[:, 2 * i].reshape(R, R).astype(BF16)
            c = zlev[:, 2 * i + 1].reshape(R, R)
            mat_c[3 + i] = jnp.where(lax.rem(lax.div(z, 1 << i), 2) == 0, c.T, c).astype(BF16)
        for m in range(1, 8):
            ys(m).wait_recv()
        u = yslice[0]
        for m in range(1, 8):
            u = u + yslice[m]
        for i in range(3):
            zsend[i, 0] = u
            u = mm(u, mat_w[3 + i])
        for i in range(3):
            zsend[i, 1] = u
        for m in range(1, 8):
            zs(m).start()

        for m in range(1, 8):
            m5_from(m).wait_recv()
        mat_w[6] = xlev[:, 0].reshape(R, R).astype(BF16)
        c = xlev[:, 1].reshape(R, R)
        mat_c[6] = jnp.where(lax.rem(x, 2) == 0, c.T, c).astype(BF16)
        c = xlev[:, 2].reshape(R, R)
        mat_c[7] = jnp.where(lax.div(x, 2) == 0, c.T, c).astype(BF16)

        for m in range(1, 8):
            zs(m).wait_recv()
            u = u + zgot[m, 1]
        xsend[0] = u
        xsend[1] = mm(u, mat_w[6])
        for m in range(1, 4):
            xs(m).start()
        side_z = [
            mm(zgot[1, 0], mat_c[3]),
            mm(zgot[2, 0] + zgot[3, 0], mat_c[4]),
            mm((zgot[4, 0] + zgot[5, 0]) + (zgot[6, 0] + zgot[7, 0]), mat_c[5]),
        ]
        for m in range(1, 4):
            xs(m).wait_recv()
        g = mm(xgot[2] + xgot[3], mat_c[7])
        g = mmt(g, mat_w[6]) + mm(xgot[1], mat_c[6])
        for i in (2, 1, 0):
            g = mmt(g, mat_w[3 + i]) + side_z[i]
        gdown[...] = g
        for m in range(1, 8):
            yd(m).start()
        fdown[y] = g

        for m in range(1, 8):
            yb(m).wait_recv()
        side_y = [
            mm(yblock[1], mat_c[0]),
            mm(yblock[2] + yblock[3], mat_c[1]),
            mm((yblock[4] + yblock[5]) + (yblock[6] + yblock[7]), mat_c[2]),
        ]
        for m in range(1, 8):
            yd_from(m).wait_recv()
        f = fdown[...].reshape(R, R)
        for level in (2, 1, 0):
            f = mmt(f, mat_w[level]) + side_y[level]
        up_field[...] = f
        c_field().start()

    @pl.when(is1)
    def _():
        c_field().wait_recv()

    weight = jnp.where(is0, core_mats[0], core_mats[2]).astype(BF16)
    c = core_mats[1]
    across = jnp.where(is0, c.T, c).astype(BF16)
    field[30] = mmt(up_field[...], weight) + mm(core_coef[...], across)

    def descend(i, carry):
        j = 14 - i
        both = mmt(field[16 + j], transfer[j])
        field[2 * j] = both[:, :R] + term[2 * j]
        field[2 * j + 1] = both[:, R:] + term[2 * j + 1]
        return carry

    descend(0, 0)
    lax.fori_loop(1, 3, descend, 0, unroll=2)
    lax.fori_loop(3, 7, descend, 0, unroll=4)
    lax.fori_loop(7, 15, descend, 0, unroll=4)

    def finish(t, carry):
        total[t] = (near[t] + dot(basis[t], field[t].astype(BF16), 1, 1)).astype(BF16)
        return carry

    lax.fori_loop(0, LEAVES, finish, 0, unroll=4)

    @pl.when(is1)
    def _():
        c_mats().wait_send()

    @pl.when(is0)
    def _():
        c_field().wait_send()

        @pl.when(y == 0)
        def _():
            for k in range(1, 8):
                m1(k).wait_send()

        for level in range(3):
            size = 2 << level

            @pl.when(lax.rem(y, size) == size // 2)
            def _():
                for c in direct_all(level):
                    c.wait_send()

        for m in range(1, 8):
            for group in (m2, m4, m5, ys, yb, zs, yd):
                group(m).wait_send()
        for m in range(1, 4):
            for group in (m3, xs):
                group(m).wait_send()


def tree(rows, pts, basis, transfer, coupling, ctrans, ccoup):
    dma = pltpu.SemaphoreType.DMA
    block = (R, R)
    return pl.pallas_call(
        tree_kernel,
        out_shape=jax.ShapeDtypeStruct((LEAVES, LEAF, R), BF16),
        in_specs=[VMEM] * 7,
        out_specs=VMEM,
        scratch_shapes=[
            pltpu.VMEM((31,) + block, F32),
            pltpu.VMEM((30,) + block, F32),
            pltpu.VMEM((31,) + block, F32),
            pltpu.VMEM((LEAVES, LEAF, R), F32),
            pltpu.VMEM((3,) + block, F32),
            pltpu.VMEM((3,) + block, F32),
            pltpu.VMEM(block, F32),
            pltpu.VMEM(block, F32),
            pltpu.VMEM((3, 2) + block, F32),
            pltpu.VMEM((8, 3, 16, R), F32),
            pltpu.VMEM((4, 3, 16, R), F32),
            pltpu.VMEM((8, 6, 16, R), F32),
            pltpu.VMEM((8, 3, 16, R), F32),
            pltpu.VMEM((7,) + block, BF16),
            pltpu.VMEM((8,) + block, BF16),
            pltpu.VMEM((4,) + block, F32),
            pltpu.VMEM((8, 16, R), F32),
            pltpu.VMEM((8,) + block, F32),
            pltpu.VMEM((3, 2, 16, R), F32),
            pltpu.VMEM((8, 2, 16, R), F32),
            pltpu.VMEM((2, 16, R), F32),
            pltpu.VMEM((4, 16, R), F32),
            pltpu.VMEM((16, R), F32),
            pltpu.VMEM((8, 16, R), F32),
            dma((3,)), dma((3,)),
            dma((8,)), dma((3,)),
            dma((8,)), dma,
            dma((8,)), dma((8,)),
            dma((4,)), dma((4,)),
            dma((8,)), dma((8,)),
            dma((8,)), dma((8,)),
            dma((8,)), dma((8,)),
            dma((8,)), dma((8,)),
            dma((8,)), dma((8,)),
            dma((4,)), dma((4,)),
            dma((8,)), dma((8,)),
        ],
        compiler_params=pltpu.CompilerParams(
            collective_id=0, has_side_effects=True, vmem_limit_bytes=VMEM_LIMIT
        ),
        name="tree",
    )(rows, pts, basis, transfer, coupling, ctrans, ccoup)


def body(
    values,
    points,
    tree_order,
    leaf_sizes,
    leaf_basis,
    local_transfer,
    local_coupling,
    cross_transfer,
    cross_coupling,
):
    rows, pts = gather(values, points, tree_order, leaf_sizes)
    transfer = local_transfer.reshape(LEAVES - 1, 2 * R, R)
    total = tree(rows, pts, leaf_basis, transfer, local_coupling, cross_transfer, cross_coupling)
    return scatter(total, tree_order, leaf_sizes)


def solution(mesh):
    in_specs = (
        P("leaf", None),
        P(None, "leaf"),
        P("leaf", None),
        P("leaf", None),
        P("leaf", None, None),
        P("leaf", None, None, None),
        P("leaf", None, None),
        P("leaf", None, None, None),
        P("leaf", None, None),
    )
    out_specs = P("leaf", None)
    return jax.shard_map(body, mesh=mesh, in_specs=in_specs, out_specs=out_specs, check_vma=False)
```

```python
import functools

import jax
import jax.numpy as jnp
from jax import lax
from jax.experimental import pallas as pl
from jax.experimental.pallas import tpu as pltpu
from jax.sharding import PartitionSpec as P

F32 = jnp.float32
BF16 = jnp.bfloat16
MESH = pl.DeviceIdType.MESH
VMEM = pl.BlockSpec(memory_space=pltpu.VMEM)
SMEM = pl.BlockSpec(memory_space=pltpu.SMEM)
HBM = pl.BlockSpec(memory_space=pl.ANY)
VMEM_LIMIT = 56 * 2**20

PTS = 3072
LEAF = 256
LEAVES = 16
R = 128
UNROLL = 32


def point_pieces(p):
    h = p.astype(BF16).astype(F32)
    rest = p - h
    m = rest.astype(BF16).astype(F32)
    low = (rest - m).astype(BF16).astype(F32)
    q = jnp.sum(p * p, axis=0, keepdims=True) * -0.125
    qh = q.astype(BF16).astype(F32)
    rest = q - qh
    qm = rest.astype(BF16).astype(F32)
    ql = (rest - qm).astype(BF16).astype(F32)
    n = p.shape[1]
    row = lax.broadcasted_iota(jnp.int32, (8, n), 0)
    parts = jnp.where(row % 3 == 0, qh, jnp.where(row % 3 == 1, qm, ql))
    left_q = jnp.where(row < 3, parts, jnp.where(row < 6, 1.0, 0.0))
    right_q = jnp.where(row < 3, 1.0, jnp.where(row < 6, parts, 0.0))
    zero = jnp.zeros((8, n), F32)
    left = [h * 0.25, h * 0.25, m * 0.25, m * 0.25, h * 0.25, low * 0.25, left_q, zero]
    right = [h, m, h, m, low, h, right_q, zero]
    return jnp.concatenate(left + right, axis=0)


def scatter_kernel(order, sizes, total, out, tree, held):
    start = 0
    for t in range(LEAVES):
        tree[pl.ds(start, LEAF), :] = total[t].astype(F32)
        start = start + sizes[0, t]

    def move(i, carry):
        base = pl.multiple_of(i * UNROLL, UNROLL)
        for u in range(UNROLL):
            held[pl.ds(order[0, base + u], 1), :] = tree[pl.ds(base + u, 1), :]
        return carry

    lax.fori_loop(0, PTS // UNROLL, move, 0)
    out[...] = held[...].astype(BF16)


def scatter(total, order, sizes):
    return pl.pallas_call(
        scatter_kernel,
        out_shape=jax.ShapeDtypeStruct((PTS, R), BF16),
        in_specs=[SMEM, SMEM, VMEM],
        out_specs=VMEM,
        scratch_shapes=[
            pltpu.VMEM((PTS + LEAF, R), F32),
            pltpu.VMEM((PTS, R), F32),
        ],
        compiler_params=pltpu.CompilerParams(vmem_limit_bytes=VMEM_LIMIT),
        name="scatter_rows",
    )(order, sizes, total)


def dot(a, b, ca=1, cb=0):
    return lax.dot_general(a, b, (((ca,), (cb,)), ((), ())), preferred_element_type=F32)


def split(x):
    h = x.astype(BF16)
    return jnp.concatenate([h, (x - h.astype(F32)).astype(BF16)], axis=0)


def mm(x, w):
    y = dot(split(x), w)
    return y[: x.shape[0]] + y[x.shape[0] :]


def mmt(x, w):
    y = dot(split(x), w, 1, 1)
    return y[: x.shape[0]] + y[x.shape[0] :]


def flip(v, m):
    out = v
    for i in range(3):
        if (m >> i) & 1:
            bit = lax.rem(lax.div(v, 2**i), 2)
            out = out + (1 - 2 * bit) * 2**i
    return out


def reach(m):
    return m.bit_length() - 1


def tree_kernel(
    order, sizes, v_ref, p_ref, basis_any, transfer_any, coupling_any, ctrans, ccoup, total,
    basis, transfer, coupling, s_local, tv, tp, gv, gp, rows, pts,
    coef, term, field, near, own, core_mats, core_coef, up_field,
    path, piece, xpiece, zlev, xlev, mat_w, mat_c,
    prod, yslice, yblock, zsend, zgot, xsend, xgot, gdown, fdown,
    s_core, r_core, s_dir, r_dir, s_m1, r_m1, s_m2, r_m2, s_m3, r_m3, s_m4, r_m4, s_m5, r_m5,
    s_ys, r_ys, s_yb, r_yb, s_z, r_z, s_x, r_x, s_yd, r_yd,
):
    me = lax.axis_index("leaf")
    core = lax.rem(me, 2)
    y = lax.rem(lax.div(me, 2), 8)
    z = lax.rem(lax.div(me, 16), 8)
    x = lax.div(me, 128)
    is0 = core == 0
    is1 = core == 1

    def at(xx, zz, yy):
        return ((xx * 8 + zz) * 8 + yy) * 2

    mate = me + 1 - 2 * core
    along_y = [at(x, z, flip(y, m)) for m in range(8)]
    along_z = [at(x, flip(z, m), y) for m in range(8)]
    along_x = [at(flip(x, m), z, y) for m in range(4)]

    def copy(src, dst, send, recv, to):
        return pltpu.make_async_remote_copy(
            src_ref=src, dst_ref=dst, send_sem=send, recv_sem=recv, device_id=(to,), device_id_type=MESH
        )

    loads = [
        pltpu.make_async_copy(src, dst, s_local.at[i])
        for i, (src, dst) in enumerate(
            [(basis_any, basis), (transfer_any, transfer), (coupling_any, coupling)]
        )
    ]
    for load in loads:
        load.start()

    own[0] = ctrans[0, 0].astype(F32)
    own[1] = ccoup[0].astype(F32)
    own[2] = ctrans[0, 1].astype(F32)

    barrier = pltpu.get_barrier_semaphore()
    pl.semaphore_signal(barrier, inc=1, device_id=(mate,), device_id_type=MESH)

    @pl.when(is0)
    def _():
        for to in along_y[1:] + along_z[1:] + along_x[1:]:
            pl.semaphore_signal(barrier, inc=1, device_id=(to,), device_id_type=MESH)

    tv[...] = v_ref[...].astype(F32)
    gv[PTS:, :] = jnp.zeros((LEAF, R), F32)
    gp[PTS:, :] = jnp.zeros((LEAF, R), F32)

    @pl.when(is0)
    def _():
        pl.semaphore_wait(barrier, 18)

    @pl.when(is1)
    def _():
        pl.semaphore_wait(barrier, 1)

    def c_mats():
        return copy(own, core_mats, s_core.at[0], r_core.at[0], mate)

    def c_coef():
        return copy(coef.at[30], core_coef, s_core.at[1], r_core.at[1], mate)

    def c_field():
        return copy(up_field, up_field, s_core.at[2], r_core.at[2], mate)


    def direct(level, i, which):
        size = 2 << level
        half = size // 2
        src = own.at[1] if which else own.at[0 if i < half else 2]
        to = at(x, z, y - half + i)
        return copy(src, path.at[level, which], s_dir.at[which, i], r_dir.at[which, level], to)

    def direct_all(level):
        size = 2 << level
        return [direct(level, i, which) for which in range(2) for i in range(size) if i != size // 2]

    def m1(k):
        return copy(own.at[:, 16 * k : 16 * k + 16, :], piece.at[z], s_m1.at[k], r_m1, at(x, z, k))

    def m2(m):
        return copy(piece.at[z], piece.at[z], s_m2.at[m], r_m2.at[m], along_z[m])

    def m2_from(m):
        there = piece.at[flip(z, m)]
        return copy(there, there, s_m2.at[m], r_m2.at[m], along_z[m])

    def m3(m):
        return copy(piece.at[0], xpiece.at[x], s_m3.at[m], r_m3.at[m], along_x[m])

    def m3_from(m):
        return copy(piece.at[0], xpiece.at[flip(x, m)], s_m3.at[m], r_m3.at[m], along_x[m])

    def m4(m):
        return copy(zlev.at[y], zlev.at[y], s_m4.at[m], r_m4.at[m], along_y[m])

    def m4_from(m):
        return copy(zlev.at[y], zlev.at[flip(y, m)], s_m4.at[m], r_m4.at[m], along_y[m])

    def m5(m):
        return copy(xlev.at[y], xlev.at[y], s_m5.at[m], r_m5.at[m], along_y[m])

    def m5_from(m):
        return copy(xlev.at[y], xlev.at[flip(y, m)], s_m5.at[m], r_m5.at[m], along_y[m])

    def ys(m):
        part = prod.at[3, pl.ds(pl.multiple_of(16 * flip(y, m), 16), 16), :]
        return copy(part, yslice.at[m], s_ys.at[m], r_ys.at[m], along_y[m])

    def yb(m):
        return copy(prod.at[reach(m)], yblock.at[m], s_yb.at[m], r_yb.at[m], along_y[m])

    def zs(m):
        return copy(zsend.at[reach(m)], zgot.at[m], s_z.at[m], r_z.at[m], along_z[m])

    def xs(m):
        return copy(xsend.at[reach(m)], xgot.at[m], s_x.at[m], r_x.at[m], along_x[m])

    def yd(m):
        return copy(gdown, fdown.at[y], s_yd.at[m], r_yd.at[m], along_y[m])

    def yd_from(m):
        return copy(gdown, fdown.at[flip(y, m)], s_yd.at[m], r_yd.at[m], along_y[m])

    @pl.when(is1)
    def _():
        c_mats().start()
        core_mats[...] = own[...]

    @pl.when(is0)
    def _():
        @pl.when(y == 0)
        def _():
            for k in range(1, 8):
                m1(k).start()
            piece[z] = own[:, 0:16, :]

        for level in range(3):
            size = 2 << level

            @pl.when(lax.rem(y, size) == size // 2)
            def _():
                for c in direct_all(level):
                    c.start()
                path[level, 0] = own[2]
                path[level, 1] = own[1]

    def permute(table, placed, first, last):
        def move(i, carry):
            base = pl.multiple_of(i * UNROLL, UNROLL)
            for u in range(UNROLL):
                placed[pl.ds(base + u, 1), :] = table[pl.ds(order[0, base + u], 1), :]
            return carry

        lax.fori_loop(first // UNROLL, last // UNROLL, move, 0)

    permute(tv, gv, 0, PTS)

    @pl.when(is0)
    def _():
        @pl.when(y > 0)
        def _():
            m1(1).wait_recv()

        for m in range(1, 8):
            m2(m).start()

    slot = lax.broadcasted_iota(jnp.int32, (LEAF, R), 0)
    starts = [0]
    for t in range(LEAVES):
        size = sizes[0, t]
        rows[t] = jnp.where(slot < size, gv[pl.ds(starts[t], LEAF), :], 0.0).astype(BF16)
        starts.append(starts[t] + size)
    loads[0].wait()
    for t in range(LEAVES):
        coef[t] = dot(rows[t], basis[t], 0, 0)
    loads[1].wait()
    for j in range(15):
        both = jnp.concatenate([coef[2 * j], coef[2 * j + 1]], axis=1)
        coef[16 + j] = mm(both, transfer[j])
    c_coef().start()

    loads[2].wait()
    for j in range(15):
        term[2 * j] = mmt(coef[2 * j + 1], coupling[j])
        term[2 * j + 1] = mm(coef[2 * j], coupling[j])

    @pl.when(is0)
    def _():
        for which in range(2):
            for level in range(3):
                size = 2 << level

                @pl.when(lax.rem(y, size) != size // 2)
                def _():
                    copy(
                        own.at[0], path.at[level, which], s_dir.at[0, 0], r_dir.at[which, level], mate
                    ).wait_recv()

                if which == 0:
                    mat_w[level] = path[level, 0].astype(BF16)
            if which == 0:
                c_mats().wait_recv()
                c_coef().wait()
                pair = jnp.concatenate([core_mats[0], core_mats[2]], axis=0).astype(BF16)
                prod[0] = mm(jnp.concatenate([coef[30], core_coef[...]], axis=1), pair)
                for level in range(3):
                    prod[level + 1] = mm(prod[level], mat_w[level])
                for m in range(1, 8):
                    ys(m).start()
                yslice[0] = prod[3, pl.ds(pl.multiple_of(16 * y, 16), 16), :]
        for level in range(3):
            c = path[level, 1]
            mat_c[level] = jnp.where(lax.rem(lax.div(y, 1 << level), 2) == 0, c.T, c).astype(BF16)

    @pl.when(is1)
    def _():
        c_coef().wait()

    for c in range(PTS // 128):
        span = slice(128 * c, 128 * (c + 1))
        tp[span, :] = point_pieces(p_ref[:, span]).T
    permute(tp, gp, 0, PTS // 4)

    @pl.when(is0)
    def _():
        for m in range(1, 8):
            m2_from(m).wait_recv()
        for m in range(1, 4):
            m3(m).start()
        xpiece[x] = piece[0]
        for i in range(3):
            half = 1 << i
            owner = lax.div(z, 2 * half) * 2 * half + half
            side = lax.rem(lax.div(z, half), 2)
            zlev[y, 2 * i] = piece[owner, 2 * side]
            zlev[y, 2 * i + 1] = piece[owner, 1]
        for m in range(1, 8):
            m4(m).start()

    permute(tp, gp, PTS // 4, PTS)

    @pl.when(is0)
    def _():
        for m in range(1, 4):
            m3_from(m).wait_recv()
        owner = lax.div(x, 2) * 2 + 1
        xlev[y, 0] = xpiece[owner, 2 * lax.rem(x, 2)]
        xlev[y, 1] = xpiece[owner, 1]
        xlev[y, 2] = xpiece[2, 1]
        for m in range(1, 8):
            m5(m).start()
        for m in range(1, 8):
            yb(m).start()

    for t in range(LEAVES):
        pts[t] = gp[pl.ds(starts[t], LEAF), :].astype(BF16)

    eye = (
        lax.broadcasted_iota(jnp.int32, (LEAF, LEAF), 0) == lax.broadcasted_iota(jnp.int32, (LEAF, LEAF), 1)
    ).astype(F32)
    shift = (
        lax.broadcasted_iota(jnp.int32, (R, R), 0) == lax.broadcasted_iota(jnp.int32, (R, R), 1) + 64
    ).astype(F32).astype(BF16)

    def nearby(t, carry):
        left = pts[t]
        right = dot(left, shift).astype(BF16)
        kernel = (jnp.exp(dot(left, right, 1, 1)) + eye).astype(BF16)
        near[t] = dot(kernel, rows[t])
        return carry

    lax.fori_loop(0, 4, nearby, 0, unroll=4)

    @pl.when(is0)
    def _():
        for m in range(1, 8):
            m4_from(m).wait_recv()
        for i in range(3):
            mat_w[3 + i] = zlev[:, 2 * i].reshape(R, R).astype(BF16)
            c = zlev[:, 2 * i + 1].reshape(R, R)
            mat_c[3 + i] = jnp.where(lax.rem(lax.div(z, 1 << i), 2) == 0, c.T, c).astype(BF16)
        for m in range(1, 8):
            ys(m).wait_recv()
        u = yslice[0]
        for m in range(1, 8):
            u = u + yslice[m]
        for i in range(3):
            zsend[i, 0] = u
            u = mm(u, mat_w[3 + i])
        for i in range(3):
            zsend[i, 1] = u
        for m in range(1, 8):
            zs(m).start()

    lax.fori_loop(4, LEAVES, nearby, 0, unroll=4)

    @pl.when(is0)
    def _():
        for m in range(1, 8):
            m5_from(m).wait_recv()
        mat_w[6] = xlev[:, 0].reshape(R, R).astype(BF16)
        c = xlev[:, 1].reshape(R, R)
        mat_c[6] = jnp.where(lax.rem(x, 2) == 0, c.T, c).astype(BF16)
        c = xlev[:, 2].reshape(R, R)
        mat_c[7] = jnp.where(lax.div(x, 2) == 0, c.T, c).astype(BF16)

        for m in range(1, 8):
            zs(m).wait_recv()
        u = zsend[0, 1]
        for m in range(1, 8):
            u = u + zgot[m, 1]
        xsend[0] = u
        xsend[1] = mm(u, mat_w[6])
        for m in range(1, 4):
            xs(m).start()
        side_z = [
            mm(zgot[1, 0], mat_c[3]),
            mm(zgot[2, 0] + zgot[3, 0], mat_c[4]),
            mm((zgot[4, 0] + zgot[5, 0]) + (zgot[6, 0] + zgot[7, 0]), mat_c[5]),
        ]
        for m in range(1, 4):
            xs(m).wait_recv()
        g = mm(xgot[2] + xgot[3], mat_c[7])
        g = mmt(g, mat_w[6]) + mm(xgot[1], mat_c[6])
        for i in (2, 1, 0):
            g = mmt(g, mat_w[3 + i]) + side_z[i]
        gdown[...] = g
        for m in range(1, 8):
            yd(m).start()
        fdown[y] = g

        for m in range(1, 8):
            yb(m).wait_recv()
        side_y = [
            mm(yblock[1], mat_c[0]),
            mm(yblock[2] + yblock[3], mat_c[1]),
            mm((yblock[4] + yblock[5]) + (yblock[6] + yblock[7]), mat_c[2]),
        ]
        for m in range(1, 8):
            yd_from(m).wait_recv()
        f = fdown[...].reshape(R, R)
        for level in (2, 1, 0):
            f = mmt(f, mat_w[level]) + side_y[level]
        up_field[...] = f
        c_field().start()

    @pl.when(is1)
    def _():
        c_field().wait_recv()

    weight = jnp.where(is0, core_mats[0], core_mats[2]).astype(BF16)
    c = core_mats[1]
    across = jnp.where(is0, c.T, c).astype(BF16)
    field[30] = mmt(up_field[...], weight) + mm(core_coef[...], across)

    for j in range(14, -1, -1):
        both = mmt(field[16 + j], transfer[j])
        field[2 * j] = both[:, :R] + term[2 * j]
        field[2 * j + 1] = both[:, R:] + term[2 * j + 1]

    for t in range(LEAVES):
        total[t] = (near[t] + dot(basis[t], field[t].astype(BF16), 1, 1)).astype(BF16)

    @pl.when(is1)
    def _():
        c_mats().wait_send()

    @pl.when(is0)
    def _():
        c_field().wait_send()

        @pl.when(y == 0)
        def _():
            for k in range(1, 8):
                m1(k).wait_send()

        for level in range(3):
            size = 2 << level

            @pl.when(lax.rem(y, size) == size // 2)
            def _():
                for c in direct_all(level):
                    c.wait_send()

        for m in range(1, 8):
            for group in (m2, m4, m5, ys, yb, zs, yd):
                group(m).wait_send()
        for m in range(1, 4):
            for group in (m3, xs):
                group(m).wait_send()


def tree(order, sizes, values, points, basis, transfer, coupling, ctrans, ccoup):
    dma = pltpu.SemaphoreType.DMA
    block = (R, R)
    return pl.pallas_call(
        tree_kernel,
        out_shape=jax.ShapeDtypeStruct((LEAVES, LEAF, R), BF16),
        in_specs=[SMEM, SMEM, VMEM, VMEM, HBM, HBM, HBM, VMEM, VMEM],
        out_specs=VMEM,
        scratch_shapes=[
            pltpu.VMEM((LEAVES, LEAF, R), BF16),
            pltpu.VMEM((LEAVES - 1, 2 * R, R), BF16),
            pltpu.VMEM((LEAVES - 1,) + block, BF16),
            dma((3,)),
            pltpu.VMEM((PTS, R), F32),
            pltpu.VMEM((PTS, R), F32),
            pltpu.VMEM((PTS + LEAF, R), F32),
            pltpu.VMEM((PTS + LEAF, R), F32),
            pltpu.VMEM((LEAVES, LEAF, R), BF16),
            pltpu.VMEM((LEAVES, LEAF, R), BF16),
            pltpu.VMEM((31,) + block, F32),
            pltpu.VMEM((30,) + block, F32),
            pltpu.VMEM((31,) + block, F32),
            pltpu.VMEM((LEAVES, LEAF, R), F32),
            pltpu.VMEM((3,) + block, F32),
            pltpu.VMEM((3,) + block, F32),
            pltpu.VMEM(block, F32),
            pltpu.VMEM(block, F32),
            pltpu.VMEM((3, 2) + block, F32),
            pltpu.VMEM((8, 3, 16, R), F32),
            pltpu.VMEM((4, 3, 16, R), F32),
            pltpu.VMEM((8, 6, 16, R), F32),
            pltpu.VMEM((8, 3, 16, R), F32),
            pltpu.VMEM((7,) + block, BF16),
            pltpu.VMEM((8,) + block, BF16),
            pltpu.VMEM((4,) + block, F32),
            pltpu.VMEM((8, 16, R), F32),
            pltpu.VMEM((8,) + block, F32),
            pltpu.VMEM((3, 2, 16, R), F32),
            pltpu.VMEM((8, 2, 16, R), F32),
            pltpu.VMEM((2, 16, R), F32),
            pltpu.VMEM((4, 16, R), F32),
            pltpu.VMEM((16, R), F32),
            pltpu.VMEM((8, 16, R), F32),
            dma((3,)), dma((3,)),
            dma((2, 8)), dma((2, 3)),
            dma((8,)), dma,
            dma((8,)), dma((8,)),
            dma((4,)), dma((4,)),
            dma((8,)), dma((8,)),
            dma((8,)), dma((8,)),
            dma((8,)), dma((8,)),
            dma((8,)), dma((8,)),
            dma((8,)), dma((8,)),
            dma((4,)), dma((4,)),
            dma((8,)), dma((8,)),
        ],
        compiler_params=pltpu.CompilerParams(
            collective_id=0, has_side_effects=True, vmem_limit_bytes=VMEM_LIMIT
        ),
        name="tree",
    )(order, sizes, values, points, basis, transfer, coupling, ctrans, ccoup)


def body(
    values,
    points,
    tree_order,
    leaf_sizes,
    leaf_basis,
    local_transfer,
    local_coupling,
    cross_transfer,
    cross_coupling,
):
    transfer = local_transfer.reshape(LEAVES - 1, 2 * R, R)
    total = tree(
        tree_order, leaf_sizes, values, points,
        leaf_basis, transfer, local_coupling, cross_transfer, cross_coupling,
    )
    return scatter(total, tree_order, leaf_sizes)


def solution(mesh):
    in_specs = (
        P("leaf", None),
        P(None, "leaf"),
        P("leaf", None),
        P("leaf", None),
        P("leaf", None, None),
        P("leaf", None, None, None),
        P("leaf", None, None),
        P("leaf", None, None, None),
        P("leaf", None, None),
    )
    out_specs = P("leaf", None)
    return jax.shard_map(body, mesh=mesh, in_specs=in_specs, out_specs=out_specs, check_vma=False)
```

```python
import functools

import jax
import jax.numpy as jnp
from jax import lax
from jax.experimental import pallas as pl
from jax.experimental.pallas import tpu as pltpu
from jax.sharding import PartitionSpec as P

F32 = jnp.float32
BF16 = jnp.bfloat16
MESH = pl.DeviceIdType.MESH
VMEM = pl.BlockSpec(memory_space=pltpu.VMEM)
SMEM = pl.BlockSpec(memory_space=pltpu.SMEM)
HBM = pl.BlockSpec(memory_space=pl.ANY)
VMEM_LIMIT = 56 * 2**20

PTS = 3072
LEAF = 256
LEAVES = 16
R = 128
UNROLL = 64


def point_pieces(p):
    h = p.astype(BF16).astype(F32)
    rest = p - h
    m = rest.astype(BF16).astype(F32)
    low = (rest - m).astype(BF16).astype(F32)
    q = jnp.sum(p * p, axis=0, keepdims=True) * -0.125
    qh = q.astype(BF16).astype(F32)
    rest = q - qh
    qm = rest.astype(BF16).astype(F32)
    ql = (rest - qm).astype(BF16).astype(F32)
    n = p.shape[1]
    row = lax.broadcasted_iota(jnp.int32, (8, n), 0)
    parts = jnp.where(row % 3 == 0, qh, jnp.where(row % 3 == 1, qm, ql))
    left_q = jnp.where(row < 3, parts, jnp.where(row < 6, 1.0, 0.0))
    right_q = jnp.where(row < 3, 1.0, jnp.where(row < 6, parts, 0.0))
    zero = jnp.zeros((8, n), F32)
    left = [h * 0.25, h * 0.25, m * 0.25, m * 0.25, h * 0.25, low * 0.25, left_q, zero]
    right = [h, m, h, m, low, h, right_q, zero]
    return jnp.concatenate(left + right, axis=0)


def scatter_kernel(order, sizes, total, out, tree, held):
    start = 0
    for t in range(LEAVES):
        tree[pl.ds(start, LEAF), :] = total[t].astype(F32)
        start = start + sizes[0, t]

    def move(i, carry):
        base = pl.multiple_of(i * UNROLL, UNROLL)
        for u in range(UNROLL):
            held[pl.ds(order[0, base + u], 1), :] = tree[pl.ds(base + u, 1), :]
        return carry

    lax.fori_loop(0, PTS // UNROLL, move, 0)
    out[...] = held[...].astype(BF16)


def scatter(total, order, sizes):
    return pl.pallas_call(
        scatter_kernel,
        out_shape=jax.ShapeDtypeStruct((PTS, R), BF16),
        in_specs=[SMEM, SMEM, VMEM],
        out_specs=VMEM,
        scratch_shapes=[
            pltpu.VMEM((PTS + LEAF, R), F32),
            pltpu.VMEM((PTS, R), F32),
        ],
        compiler_params=pltpu.CompilerParams(vmem_limit_bytes=VMEM_LIMIT),
        name="scatter_rows",
    )(order, sizes, total)


def dot(a, b, ca=1, cb=0):
    return lax.dot_general(a, b, (((ca,), (cb,)), ((), ())), preferred_element_type=F32)


def split(x):
    h = x.astype(BF16)
    return jnp.concatenate([h, (x - h.astype(F32)).astype(BF16)], axis=0)


def mm(x, w):
    y = dot(split(x), w)
    return y[: x.shape[0]] + y[x.shape[0] :]


def mmt(x, w):
    y = dot(split(x), w, 1, 1)
    return y[: x.shape[0]] + y[x.shape[0] :]


def flip(v, m):
    out = v
    for i in range(3):
        if (m >> i) & 1:
            bit = lax.rem(lax.div(v, 2**i), 2)
            out = out + (1 - 2 * bit) * 2**i
    return out


def reach(m):
    return m.bit_length() - 1


def tree_kernel(
    order, sizes, v_ref, p_ref, basis_any, transfer_any, coupling_any, ctrans, ccoup, total,
    v_in, p_in, basis, transfer, coupling, s_local, tv, tp, gv, gp, rows, pts,
    coef, term, field, near, own, core_mats, core_coef, up_field,
    path, piece, wpiece, wlev, xpiece, xpath, xlev, mat_w, mat_c,
    prod, yslice, yblock, zsend, zgot, xsend, xgot, gdown, fdown,
    s_core, r_core, s_dir, r_dir, s_m1, r_m1, s_mw, r_mw, s_m4w, r_m4w, s_m2, r_m2, s_m3, r_m3, s_mx, r_mx, s_m5, r_m5,
    s_ys, r_ys, s_yb, r_yb, s_z, r_z, s_x, r_x, s_yd, r_yd,
):
    me = lax.axis_index("leaf")
    core = lax.rem(me, 2)
    y = lax.rem(lax.div(me, 2), 8)
    z = lax.rem(lax.div(me, 16), 8)
    x = lax.div(me, 128)
    is0 = core == 0
    is1 = core == 1

    def at(xx, zz, yy):
        return ((xx * 8 + zz) * 8 + yy) * 2

    mate = me + 1 - 2 * core
    along_y = [at(x, z, flip(y, m)) for m in range(8)]
    along_z = [at(x, flip(z, m), y) for m in range(8)]
    along_x = [at(flip(x, m), z, y) for m in range(4)]

    def copy(src, dst, send, recv, to):
        return pltpu.make_async_remote_copy(
            src_ref=src, dst_ref=dst, send_sem=send, recv_sem=recv, device_id=(to,), device_id_type=MESH
        )

    loads = [
        pltpu.make_async_copy(src, dst, s_local.at[i])
        for i, (src, dst) in enumerate(
            [(v_ref, v_in), (p_ref, p_in), (basis_any, basis), (transfer_any, transfer), (coupling_any, coupling)]
        )
    ]
    for load in loads:
        load.start()

    own[0] = ctrans[0, 0].astype(F32)
    own[1] = ccoup[0].astype(F32)
    own[2] = ctrans[0, 1].astype(F32)

    barrier = pltpu.get_barrier_semaphore()
    pl.semaphore_signal(barrier, inc=1, device_id=(mate,), device_id_type=MESH)

    @pl.when(is0)
    def _():
        for to in along_y[1:] + along_z[1:] + along_x[1:]:
            pl.semaphore_signal(barrier, inc=1, device_id=(to,), device_id_type=MESH)

    loads[0].wait()
    tv[...] = v_in[...].astype(F32)
    gv[PTS:, :] = jnp.zeros((LEAF, R), F32)
    gp[PTS:, :] = jnp.zeros((LEAF, R), F32)

    @pl.when(is0)
    def _():
        pl.semaphore_wait(barrier, 18)

    @pl.when(is1)
    def _():
        pl.semaphore_wait(barrier, 1)

    def c_mats():
        return copy(own, core_mats, s_core.at[0], r_core.at[0], mate)

    def c_coef():
        return copy(coef.at[30], core_coef, s_core.at[1], r_core.at[1], mate)

    def c_field():
        return copy(up_field, up_field, s_core.at[2], r_core.at[2], mate)


    def direct(level, i, which):
        size = 2 << level
        half = size // 2
        src = own.at[1] if which else own.at[0 if i < half else 2]
        to = at(x, z, y - half + i)
        return copy(src, path.at[level, which], s_dir.at[which, i], r_dir.at[which, level], to)

    def direct_all(level, which):
        size = 2 << level
        return [direct(level, i, which) for i in range(size) if i != size // 2]

    def m1(k):
        return copy(own.at[:, 16 * k : 16 * k + 16, :], piece.at[z], s_m1.at[k], r_m1, at(x, z, k))

    def mw(m):
        to = flip(z, m)
        side = jnp.where(to < z, 0, 2)
        return copy(piece.at[z, side], wpiece.at[z], s_mw.at[m], r_mw.at[m], along_z[m])

    def mw_from(m):
        return copy(piece.at[z, 0], wpiece.at[flip(z, m)], s_mw.at[m], r_mw.at[m], along_z[m])

    def m4w(m):
        return copy(wlev.at[y], wlev.at[y], s_m4w.at[m], r_m4w.at[m], along_y[m])

    def m4w_from(m):
        return copy(wlev.at[y], wlev.at[flip(y, m)], s_m4w.at[m], r_m4w.at[m], along_y[m])

    def m2(m):
        return copy(piece.at[z, 1], piece.at[z, 1], s_m2.at[m], r_m2.at[m], along_z[m])

    def m2_from(m):
        there = piece.at[flip(z, m), 1]
        return copy(there, there, s_m2.at[m], r_m2.at[m], along_z[m])

    def m3(m):
        return copy(piece.at[0], xpiece.at[x], s_m3.at[m], r_m3.at[m], along_x[m])

    def mx(m):
        return copy(xpath, xpath, s_mx.at[m], r_mx, at(x, m, y))

    def m3_from(m):
        return copy(piece.at[0], xpiece.at[flip(x, m)], s_m3.at[m], r_m3.at[m], along_x[m])

    def m5(m):
        return copy(xlev.at[y], xlev.at[y], s_m5.at[m], r_m5.at[m], along_y[m])

    def m5_from(m):
        return copy(xlev.at[y], xlev.at[flip(y, m)], s_m5.at[m], r_m5.at[m], along_y[m])

    def ys(m):
        part = prod.at[3, pl.ds(pl.multiple_of(16 * flip(y, m), 16), 16), :]
        return copy(part, yslice.at[m], s_ys.at[m], r_ys.at[m], along_y[m])

    def yb(m):
        return copy(prod.at[reach(m)], yblock.at[m], s_yb.at[m], r_yb.at[m], along_y[m])

    def zs(m):
        return copy(zsend.at[reach(m)], zgot.at[m], s_z.at[m], r_z.at[m], along_z[m])

    def xs(m):
        return copy(xsend.at[reach(m)], xgot.at[m], s_x.at[m], r_x.at[m], along_x[m])

    def yd(m):
        return copy(gdown, fdown.at[y], s_yd.at[m], r_yd.at[m], along_y[m])

    def yd_from(m):
        return copy(gdown, fdown.at[flip(y, m)], s_yd.at[m], r_yd.at[m], along_y[m])

    @pl.when(is1)
    def _():
        c_mats().start()
        core_mats[...] = own[...]

    @pl.when(is0)
    def _():
        @pl.when(y == 0)
        def _():
            for k in range(1, 8):
                m1(k).start()
            piece[z] = own[:, 0:16, :]

        for level in range(3):
            size = 2 << level

            @pl.when(lax.rem(y, size) == size // 2)
            def _():
                for c in direct_all(level, 0):
                    c.start()
                path[level, 0] = own[2]
                path[level, 1] = own[1]

    def wait_path(which):
        for level in range(3):
            size = 2 << level

            @pl.when(lax.rem(y, size) != size // 2)
            def _():
                got = path.at[level, which]
                copy(own.at[0], got, s_dir.at[0, 0], r_dir.at[which, level], mate).wait_recv()

    def permute(table, placed, first, last):
        def move(i, carry):
            base = pl.multiple_of(i * UNROLL, UNROLL)
            for u in range(UNROLL):
                placed[pl.ds(base + u, 1), :] = table[pl.ds(order[0, base + u], 1), :]
            return carry

        lax.fori_loop(first // UNROLL, last // UNROLL, move, 0)

    permute(tv, gv, 0, PTS)

    slot = lax.broadcasted_iota(jnp.int32, (LEAF, R), 0)
    starts = [0]
    for t in range(LEAVES):
        size = sizes[0, t]
        rows[t] = jnp.where(slot < size, gv[pl.ds(starts[t], LEAF), :], 0.0).astype(BF16)
        starts.append(starts[t] + size)
    loads[2].wait()
    for t in range(LEAVES):
        coef[t] = dot(rows[t], basis[t], 0, 0)
    loads[3].wait()
    for j in range(15):
        both = jnp.concatenate([coef[2 * j], coef[2 * j + 1]], axis=1)
        coef[16 + j] = mm(both, transfer[j])
    c_coef().start()

    @pl.when(is0)
    def _():
        @pl.when(y > 0)
        def _():
            m1(1).wait_recv()

        for m in range(1, 8):
            mw(m).start()
        for m in range(1, 8):
            m2(m).start()
        wpiece[z] = piece[z, 2]

        @pl.when(z == 0)
        def _():
            for m in range(1, 4):
                m3(m).start()
            xpiece[x] = piece[0]

    loads[4].wait()
    for j in range(15):
        term[2 * j] = mmt(coef[2 * j + 1], coupling[j])
        term[2 * j + 1] = mm(coef[2 * j], coupling[j])

    @pl.when(is0)
    def _():
        wait_path(0)
        for level in range(3):
            mat_w[level] = path[level, 0].astype(BF16)
        c_mats().wait_recv()
        c_coef().wait()
        pair = jnp.concatenate([core_mats[0], core_mats[2]], axis=0).astype(BF16)
        prod[0] = mm(jnp.concatenate([coef[30], core_coef[...]], axis=1), pair)
        for level in range(3):
            prod[level + 1] = mm(prod[level], mat_w[level])
        for m in range(1, 8):
            ys(m).start()
        for lev in range(3):

            @pl.when(lax.rem(y, 2 << lev) == 1 << lev)
            def _():
                for c in direct_all(lev, 1):
                    c.start()

        yslice[0] = prod[3, pl.ds(pl.multiple_of(16 * y, 16), 16), :]

    @pl.when(is1)
    def _():
        c_coef().wait()

    loads[1].wait()
    for c in range(PTS // 128):
        span = slice(128 * c, 128 * (c + 1))
        tp[span, :] = point_pieces(p_in[:, span]).T
    @pl.when(jnp.logical_and(is0, z == 0))
    def _():
        for m in range(1, 4):
            m3_from(m).wait_recv()
        owner = lax.div(x, 2) * 2 + 1
        xpath[0] = xpiece[owner, 1]
        xpath[1] = xpiece[2, 1]
        xpath[2] = xpiece[owner, 2 * lax.rem(x, 2)]
        for m in range(1, 8):
            mx(m).start()

    permute(tp, gp, 0, PTS // 2)

    @pl.when(is0)
    def _():
        for m in range(1, 8):
            mw_from(m).wait_recv()
        for i in range(3):
            wlev[y, i] = wpiece[lax.div(z, 2 << i) * (2 << i) + (1 << i)]
        for m in range(1, 8):
            m4w(m).start()

    permute(tp, gp, PTS // 2, PTS)

    for t in range(LEAVES):
        pts[t] = gp[pl.ds(starts[t], LEAF), :].astype(BF16)

    eye = (
        lax.broadcasted_iota(jnp.int32, (LEAF, LEAF), 0) == lax.broadcasted_iota(jnp.int32, (LEAF, LEAF), 1)
    ).astype(F32)
    shift = (
        lax.broadcasted_iota(jnp.int32, (R, R), 0) == lax.broadcasted_iota(jnp.int32, (R, R), 1) + 64
    ).astype(F32).astype(BF16)

    def nearby(t, carry):
        left = pts[t]
        right = dot(left, shift).astype(BF16)
        kernel = (jnp.exp(dot(left, right, 1, 1)) + eye).astype(BF16)
        near[t] = dot(kernel, rows[t])
        return carry

    lax.fori_loop(0, 4, nearby, 0, unroll=4)

    @pl.when(is0)
    def _():
        for m in range(1, 8):
            m2_from(m).wait_recv()

        @pl.when(z > 0)
        def _():
            mx(1).wait_recv()

        for i in range(3):
            xlev[y, i] = piece[lax.div(z, 2 << i) * (2 << i) + (1 << i), 1]
        xlev[y, 3:6] = xpath[...]
        for m in range(1, 8):
            m5(m).start()
        for m in range(1, 8):
            yb(m).start()

    @pl.when(is0)
    def _():
        for m in range(1, 8):
            m4w_from(m).wait_recv()
        for i in range(3):
            mat_w[3 + i] = wlev[:, i].reshape(R, R).astype(BF16)
        for m in range(1, 8):
            ys(m).wait_recv()
        u = yslice[0]
        for m in range(1, 8):
            u = u + yslice[m]
        for i in range(3):
            zsend[i, 0] = u
            u = mm(u, mat_w[3 + i])
        for i in range(3):
            zsend[i, 1] = u
        for m in range(1, 8):
            zs(m).start()

    lax.fori_loop(4, LEAVES, nearby, 0, unroll=4)

    @pl.when(is0)
    def _():
        for m in range(1, 8):
            m5_from(m).wait_recv()
        mat_w[6] = xlev[:, 5].reshape(R, R).astype(BF16)

        for m in range(1, 8):
            zs(m).wait_recv()
        u = zsend[0, 1]
        for m in range(1, 8):
            u = u + zgot[m, 1]
        xsend[0] = u
        xsend[1] = mm(u, mat_w[6])
        for m in range(1, 4):
            xs(m).start()
        sides = [lax.rem(lax.div(z, 1 << i), 2) for i in range(3)] + [lax.rem(x, 2), lax.div(x, 2)]
        for i in range(5):
            c = xlev[:, i].reshape(R, R)
            mat_c[3 + i] = jnp.where(sides[i] == 0, c.T, c).astype(BF16)
        side_z = [
            mm(zgot[1, 0], mat_c[3]),
            mm(zgot[2, 0] + zgot[3, 0], mat_c[4]),
            mm((zgot[4, 0] + zgot[5, 0]) + (zgot[6, 0] + zgot[7, 0]), mat_c[5]),
        ]
        for m in range(1, 4):
            xs(m).wait_recv()
        g = mm(xgot[2] + xgot[3], mat_c[7])
        g = mmt(g, mat_w[6]) + mm(xgot[1], mat_c[6])
        for i in (2, 1, 0):
            g = mmt(g, mat_w[3 + i]) + side_z[i]
        gdown[...] = g
        for m in range(1, 8):
            yd(m).start()
        fdown[y] = g

        wait_path(1)
        for level in range(3):
            c = path[level, 1]
            mat_c[level] = jnp.where(lax.rem(lax.div(y, 1 << level), 2) == 0, c.T, c).astype(BF16)
        for m in range(1, 8):
            yb(m).wait_recv()
        side_y = [
            mm(yblock[1], mat_c[0]),
            mm(yblock[2] + yblock[3], mat_c[1]),
            mm((yblock[4] + yblock[5]) + (yblock[6] + yblock[7]), mat_c[2]),
        ]
        for m in range(1, 8):
            yd_from(m).wait_recv()
        f = fdown[...].reshape(R, R)
        for level in (2, 1, 0):
            f = mmt(f, mat_w[level]) + side_y[level]
        up_field[...] = f
        c_field().start()

    @pl.when(is1)
    def _():
        c_field().wait_recv()

    weight = jnp.where(is0, core_mats[0], core_mats[2]).astype(BF16)
    c = core_mats[1]
    across = jnp.where(is0, c.T, c).astype(BF16)
    field[30] = mmt(up_field[...], weight) + mm(core_coef[...], across)

    for j in range(14, -1, -1):
        both = mmt(field[16 + j], transfer[j])
        field[2 * j] = both[:, :R] + term[2 * j]
        field[2 * j + 1] = both[:, R:] + term[2 * j + 1]

    for t in range(LEAVES):
        total[t] = (near[t] + dot(basis[t], field[t].astype(BF16), 1, 1)).astype(BF16)

    @pl.when(is1)
    def _():
        c_mats().wait_send()

    @pl.when(is0)
    def _():
        c_field().wait_send()

        @pl.when(y == 0)
        def _():
            for k in range(1, 8):
                m1(k).wait_send()

        for level in range(3):
            size = 2 << level

            @pl.when(lax.rem(y, size) == size // 2)
            def _():
                for c in direct_all(level, 0) + direct_all(level, 1):
                    c.wait_send()

        for m in range(1, 8):
            for group in (mw, m4w, m2, m5, ys, yb, zs, yd):
                group(m).wait_send()
        for m in range(1, 4):
            xs(m).wait_send()

        @pl.when(z == 0)
        def _():
            for m in range(1, 4):
                m3(m).wait_send()
            for m in range(1, 8):
                mx(m).wait_send()


def tree(order, sizes, values, points, basis, transfer, coupling, ctrans, ccoup):
    dma = pltpu.SemaphoreType.DMA
    block = (R, R)
    return pl.pallas_call(
        tree_kernel,
        out_shape=jax.ShapeDtypeStruct((LEAVES, LEAF, R), BF16),
        in_specs=[SMEM, SMEM, HBM, HBM, HBM, HBM, HBM, VMEM, VMEM],
        out_specs=VMEM,
        scratch_shapes=[
            pltpu.VMEM((PTS, R), BF16),
            pltpu.VMEM((8, PTS), F32),
            pltpu.VMEM((LEAVES, LEAF, R), BF16),
            pltpu.VMEM((LEAVES - 1, 2 * R, R), BF16),
            pltpu.VMEM((LEAVES - 1,) + block, BF16),
            dma((5,)),
            pltpu.VMEM((PTS, R), F32),
            pltpu.VMEM((PTS, R), F32),
            pltpu.VMEM((PTS + LEAF, R), F32),
            pltpu.VMEM((PTS + LEAF, R), F32),
            pltpu.VMEM((LEAVES, LEAF, R), BF16),
            pltpu.VMEM((LEAVES, LEAF, R), BF16),
            pltpu.VMEM((31,) + block, F32),
            pltpu.VMEM((30,) + block, F32),
            pltpu.VMEM((31,) + block, F32),
            pltpu.VMEM((LEAVES, LEAF, R), F32),
            pltpu.VMEM((3,) + block, F32),
            pltpu.VMEM((3,) + block, F32),
            pltpu.VMEM(block, F32),
            pltpu.VMEM(block, F32),
            pltpu.VMEM((3, 2) + block, F32),
            pltpu.VMEM((8, 3, 16, R), F32),
            pltpu.VMEM((8, 16, R), F32),
            pltpu.VMEM((8, 3, 16, R), F32),
            pltpu.VMEM((4, 3, 16, R), F32),
            pltpu.VMEM((3, 16, R), F32),
            pltpu.VMEM((8, 6, 16, R), F32),
            pltpu.VMEM((7,) + block, BF16),
            pltpu.VMEM((8,) + block, BF16),
            pltpu.VMEM((4,) + block, F32),
            pltpu.VMEM((8, 16, R), F32),
            pltpu.VMEM((8,) + block, F32),
            pltpu.VMEM((3, 2, 16, R), F32),
            pltpu.VMEM((8, 2, 16, R), F32),
            pltpu.VMEM((2, 16, R), F32),
            pltpu.VMEM((4, 16, R), F32),
            pltpu.VMEM((16, R), F32),
            pltpu.VMEM((8, 16, R), F32),
            dma((3,)), dma((3,)),
            dma((2, 8)), dma((2, 3)),
            dma((8,)), dma,
            dma((8,)), dma((8,)),
            dma((8,)), dma((8,)),
            dma((8,)), dma((8,)),
            dma((4,)), dma((4,)),
            dma((8,)), dma,
            dma((8,)), dma((8,)),
            dma((8,)), dma((8,)),
            dma((8,)), dma((8,)),
            dma((8,)), dma((8,)),
            dma((4,)), dma((4,)),
            dma((8,)), dma((8,)),
        ],
        compiler_params=pltpu.CompilerParams(
            collective_id=0, has_side_effects=True, vmem_limit_bytes=VMEM_LIMIT
        ),
        name="tree",
    )(order, sizes, values, points, basis, transfer, coupling, ctrans, ccoup)


def body(
    values,
    points,
    tree_order,
    leaf_sizes,
    leaf_basis,
    local_transfer,
    local_coupling,
    cross_transfer,
    cross_coupling,
):
    transfer = local_transfer.reshape(LEAVES - 1, 2 * R, R)
    total = tree(
        tree_order, leaf_sizes, values, points,
        leaf_basis, transfer, local_coupling, cross_transfer, cross_coupling,
    )
    return scatter(total, tree_order, leaf_sizes)


def solution(mesh):
    in_specs = (
        P("leaf", None),
        P(None, "leaf"),
        P("leaf", None),
        P("leaf", None),
        P("leaf", None, None),
        P("leaf", None, None, None),
        P("leaf", None, None),
        P("leaf", None, None, None),
        P("leaf", None, None),
    )
    out_specs = P("leaf", None)
    return jax.shard_map(body, mesh=mesh, in_specs=in_specs, out_specs=out_specs, check_vma=False)
```

```python
import functools

import jax
import jax.numpy as jnp
from jax import lax
from jax.experimental import pallas as pl
from jax.experimental.pallas import tpu as pltpu
from jax.sharding import PartitionSpec as P

F32 = jnp.float32
BF16 = jnp.bfloat16
MESH = pl.DeviceIdType.MESH
VMEM = pl.BlockSpec(memory_space=pltpu.VMEM)
SMEM = pl.BlockSpec(memory_space=pltpu.SMEM)
HBM = pl.BlockSpec(memory_space=pl.ANY)
VMEM_LIMIT = 56 * 2**20

PTS = 3072
LEAF = 256
LEAVES = 16
R = 128
UNROLL = 128
FAR_FIRST = (4, 5, 3, 7, 6, 2, 1)


def point_pieces(p):
    h = p.astype(BF16).astype(F32)
    rest = p - h
    m = rest.astype(BF16).astype(F32)
    low = (rest - m).astype(BF16).astype(F32)
    q = jnp.sum(p * p, axis=0, keepdims=True) * -0.125
    qh = q.astype(BF16).astype(F32)
    rest = q - qh
    qm = rest.astype(BF16).astype(F32)
    ql = (rest - qm).astype(BF16).astype(F32)
    n = p.shape[1]
    row = lax.broadcasted_iota(jnp.int32, (8, n), 0)
    parts = jnp.where(row % 3 == 0, qh, jnp.where(row % 3 == 1, qm, ql))
    left_q = jnp.where(row < 3, parts, jnp.where(row < 6, 1.0, 0.0))
    right_q = jnp.where(row < 3, 1.0, jnp.where(row < 6, parts, 0.0))
    zero = jnp.zeros((8, n), F32)
    left = [h * 0.25, h * 0.25, m * 0.25, m * 0.25, h * 0.25, low * 0.25, left_q, zero]
    right = [h, m, h, m, low, h, right_q, zero]
    return jnp.concatenate(left + right, axis=0)


def scatter_kernel(order, sizes, total, out, tree, held):
    start = 0
    for t in range(LEAVES):
        tree[pl.ds(start, LEAF), :] = total[t].astype(F32)
        start = start + sizes[0, t]

    def move(i, carry):
        base = pl.multiple_of(i * UNROLL, UNROLL)
        for u in range(UNROLL):
            held[pl.ds(order[0, base + u], 1), :] = tree[pl.ds(base + u, 1), :]
        return carry

    lax.fori_loop(0, PTS // UNROLL, move, 0)
    out[...] = held[...].astype(BF16)


def scatter(total, order, sizes):
    return pl.pallas_call(
        scatter_kernel,
        out_shape=jax.ShapeDtypeStruct((PTS, R), BF16),
        in_specs=[SMEM, SMEM, VMEM],
        out_specs=VMEM,
        scratch_shapes=[
            pltpu.VMEM((PTS + LEAF, R), F32),
            pltpu.VMEM((PTS, R), F32),
        ],
        compiler_params=pltpu.CompilerParams(vmem_limit_bytes=56 * 2**20),
        name="scatter_rows",
    )(order, sizes, total)


def dot(a, b, ca=1, cb=0):
    return lax.dot_general(a, b, (((ca,), (cb,)), ((), ())), preferred_element_type=F32)


def split(x):
    h = x.astype(BF16)
    return jnp.concatenate([h, (x - h.astype(F32)).astype(BF16)], axis=0)


def mm(x, w):
    y = dot(split(x), w)
    return y[: x.shape[0]] + y[x.shape[0] :]


def mmt(x, w):
    y = dot(split(x), w, 1, 1)
    return y[: x.shape[0]] + y[x.shape[0] :]


def mmt3(x, w):
    h = w.astype(BF16)
    return mmt(x, h) + dot(x.astype(BF16), (w - h.astype(F32)).astype(BF16), 1, 1)


def mm3(x, w):
    h = w.astype(BF16)
    return mm(x, h) + dot(x.astype(BF16), (w - h.astype(F32)).astype(BF16))


def exact_mmt(x, w):
    h = w.astype(BF16)
    return dot(x, h, 1, 1) + dot(x, (w - h.astype(F32)).astype(BF16), 1, 1)


def exact_mm(x, w):
    h = w.astype(BF16)
    return dot(x, h) + dot(x, (w - h.astype(F32)).astype(BF16))


def flip(v, m):
    out = v
    for i in range(3):
        if (m >> i) & 1:
            bit = lax.rem(lax.div(v, 2**i), 2)
            out = out + (1 - 2 * bit) * 2**i
    return out


def reach(m):
    return m.bit_length() - 1


def tree_kernel(
    order, sizes, v_ref, p_ref, basis_any, transfer_any, coupling_any, ctrans, ccoup, total,
    v_in, p_in, basis, transfer, coupling, s_local, tv, tp, gv, gp, rows, pts,
    coef, term, field, near, own, core_mats, core_coef, up_field,
    path, piece, wpiece, wlev, xpiece, xpath, xlev, mat_w, mat_c,
    far, prod, yslice, yblock, zsend, zgot, xsend, xgot, gdown, fdown,
    s_core, r_core, s_dir, r_dir, s_m1, r_m1, s_mw, r_mw, s_m4w, r_m4w, s_m2, r_m2, s_m3, r_m3, s_mx, r_mx, s_m5, r_m5,
    s_ys, r_ys, s_yb, r_yb, s_z, r_z, s_x, r_x, s_yd, r_yd,
):
    me = lax.axis_index("leaf")
    core = lax.rem(me, 2)
    y = lax.rem(lax.div(me, 2), 8)
    z = lax.rem(lax.div(me, 16), 8)
    x = lax.div(me, 128)
    is0 = core == 0
    is1 = core == 1

    def at(xx, zz, yy):
        return ((xx * 8 + zz) * 8 + yy) * 2

    mate = me + 1 - 2 * core
    along_y = [at(x, z, flip(y, m)) for m in range(8)]
    along_z = [at(x, flip(z, m), y) for m in range(8)]
    along_x = [at(flip(x, m), z, y) for m in range(4)]

    def copy(src, dst, send, recv, to):
        return pltpu.make_async_remote_copy(
            src_ref=src, dst_ref=dst, send_sem=send, recv_sem=recv, device_id=(to,), device_id_type=MESH
        )

    barrier = pltpu.get_barrier_semaphore()
    pl.semaphore_signal(barrier, inc=1, device_id=(mate,), device_id_type=MESH)

    @pl.when(is0)
    def _():
        for to in along_y[1:] + along_z[1:] + along_x[1:]:
            pl.semaphore_signal(barrier, inc=1, device_id=(to,), device_id_type=MESH)

    loads = [
        pltpu.make_async_copy(src, dst, s_local.at[i])
        for i, (src, dst) in enumerate(
            [(v_ref, v_in), (p_ref, p_in), (basis_any, basis), (transfer_any, transfer), (coupling_any, coupling)]
        )
    ]
    for load in loads:
        load.start()

    own[0] = ctrans[0, 0].astype(F32)
    own[1] = ccoup[0].astype(F32)
    own[2] = ctrans[0, 1].astype(F32)

    loads[0].wait()
    tv[...] = v_in[...].astype(F32)
    gv[PTS:, :] = jnp.zeros((LEAF, R), F32)
    gp[PTS:, :] = jnp.zeros((LEAF, R), F32)

    @pl.when(is0)
    def _():
        pl.semaphore_wait(barrier, 18)

    @pl.when(is1)
    def _():
        pl.semaphore_wait(barrier, 1)

    def c_mats():
        return copy(own, core_mats, s_core.at[0], r_core.at[0], mate)

    def c_coef():
        return copy(coef.at[30], core_coef, s_core.at[1], r_core.at[1], mate)

    def c_field():
        return copy(up_field, field.at[30], s_core.at[2], r_core.at[2], mate)


    def direct(level, i, which):
        size = 2 << level
        half = size // 2
        src = own.at[1] if which else own.at[0 if i < half else 2]
        to = at(x, z, y - half + i)
        return copy(src, path.at[level, which], s_dir.at[which, i], r_dir.at[which, level], to)

    def direct_all(level, which):
        size = 2 << level
        return [direct(level, i, which) for i in range(size) if i != size // 2]

    def m1(k):
        return copy(own.at[:, 16 * k : 16 * k + 16, :], piece.at[z], s_m1.at[k], r_m1, at(x, z, k))

    def mw(m):
        to = flip(z, m)
        side = jnp.where(to < z, 0, 2)
        return copy(piece.at[z, side], wpiece.at[z], s_mw.at[m], r_mw.at[m], along_z[m])

    def mw_from(m):
        return copy(piece.at[z, 0], wpiece.at[flip(z, m)], s_mw.at[m], r_mw.at[m], along_z[m])

    def m4w(m):
        return copy(wlev.at[y], wlev.at[y], s_m4w.at[m], r_m4w.at[m], along_y[m])

    def m4w_from(m):
        return copy(wlev.at[y], wlev.at[flip(y, m)], s_m4w.at[m], r_m4w.at[m], along_y[m])

    def m2(m):
        return copy(piece.at[z, 1], piece.at[z, 1], s_m2.at[m], r_m2.at[m], along_z[m])

    def m2_from(m):
        there = piece.at[flip(z, m), 1]
        return copy(there, there, s_m2.at[m], r_m2.at[m], along_z[m])

    def m3(m):
        return copy(piece.at[0], xpiece.at[x], s_m3.at[m], r_m3.at[m], along_x[m])

    def mx(m):
        return copy(xpath, xpath, s_mx.at[m], r_mx, at(x, m, y))

    def m3_from(m):
        return copy(piece.at[0], xpiece.at[flip(x, m)], s_m3.at[m], r_m3.at[m], along_x[m])

    def m5(m):
        return copy(xlev.at[y], xlev.at[y], s_m5.at[m], r_m5.at[m], along_y[m])

    def m5_from(m):
        return copy(xlev.at[y], xlev.at[flip(y, m)], s_m5.at[m], r_m5.at[m], along_y[m])

    def ys(m):
        part = prod.at[3, pl.ds(pl.multiple_of(16 * flip(y, m), 16), 16), :]
        return copy(part, yslice.at[m], s_ys.at[m], r_ys.at[m], along_y[m])

    def yb(m):
        return copy(prod.at[reach(m)], yblock.at[m], s_yb.at[m], r_yb.at[m], along_y[m])

    def zs(m):
        return copy(zsend.at[reach(m)], zgot.at[m], s_z.at[m], r_z.at[m], along_z[m])

    def xs(m):
        return copy(xsend.at[reach(m)], xgot.at[m], s_x.at[m], r_x.at[m], along_x[m])

    def yd(m):
        return copy(gdown, fdown.at[y], s_yd.at[m], r_yd.at[m], along_y[m])

    def yd_from(m):
        return copy(gdown, fdown.at[flip(y, m)], s_yd.at[m], r_yd.at[m], along_y[m])

    @pl.when(is1)
    def _():
        c_mats().start()

    @pl.when(is0)
    def _():
        @pl.when(y == 0)
        def _():
            for k in (4, 3, 5, 2, 6, 1, 7):
                m1(k).start()
            piece[z] = own[:, 0:16, :]

        for level in range(3):
            size = 2 << level

            @pl.when(lax.rem(y, size) == size // 2)
            def _():
                for c in direct_all(level, 0):
                    c.start()
                path[level, 0] = own[2]
                path[level, 1] = own[1]

    def wait_path(which):
        for level in range(3):
            size = 2 << level

            @pl.when(lax.rem(y, size) != size // 2)
            def _():
                got = path.at[level, which]
                copy(own.at[0], got, s_dir.at[0, 0], r_dir.at[which, level], mate).wait_recv()

    def permute(table, placed, first, last):
        def move(i, carry):
            base = pl.multiple_of(i * UNROLL, UNROLL)
            for u in range(UNROLL):
                placed[pl.ds(base + u, 1), :] = table[pl.ds(order[0, base + u], 1), :]
            return carry

        lax.fori_loop(first // UNROLL, last // UNROLL, move, 0)

    permute(tv, gv, 0, PTS)

    slot = lax.broadcasted_iota(jnp.int32, (LEAF, R), 0)
    starts = [0]
    for t in range(LEAVES):
        size = sizes[0, t]
        rows[t] = jnp.where(slot < size, gv[pl.ds(starts[t], LEAF), :], 0.0).astype(BF16)
        starts.append(starts[t] + size)
    loads[2].wait()
    for t in range(LEAVES):
        coef[t] = dot(rows[t], basis[t], 0, 0)
    loads[3].wait()
    for j in range(15):
        both = jnp.concatenate([coef[2 * j], coef[2 * j + 1]], axis=1)
        coef[16 + j] = mm(both, transfer[j])
    c_coef().start()

    @pl.when(is0)
    def _():
        @pl.when(y > 0)
        def _():
            m1(1).wait_recv()

        for m in FAR_FIRST:
            mw(m).start()
        for m in FAR_FIRST:
            m2(m).start()
        wpiece[z] = piece[z, 2]

        @pl.when(z == 0)
        def _():
            for m in (2, 3, 1):
                m3(m).start()
            xpiece[x] = piece[0]

    loads[4].wait()
    for j in range(15):
        term[2 * j] = mmt(coef[2 * j + 1], coupling[j])
        term[2 * j + 1] = mm(coef[2 * j], coupling[j])

    @pl.when(is0)
    def _():
        wait_path(0)
        for level in range(3):
            mat_w[level] = path[level, 0].astype(BF16)
        c_mats().wait_recv()
        c_coef().wait()
        pair = jnp.concatenate([core_mats[0], core_mats[2]], axis=0).astype(BF16)
        prod[0] = mm(jnp.concatenate([coef[30], core_coef[...]], axis=1), pair)
        for level in range(3):
            prod[level + 1] = mm(prod[level], mat_w[level])
        for m in FAR_FIRST:
            ys(m).start()
        for lev in range(3):

            @pl.when(lax.rem(y, 2 << lev) == 1 << lev)
            def _():
                for c in direct_all(lev, 1):
                    c.start()

        yslice[0] = prod[3, pl.ds(pl.multiple_of(16 * y, 16), 16), :]

    @pl.when(is1)
    def _():
        c_coef().wait()

    loads[1].wait()
    for c in range(PTS // 128):
        span = slice(128 * c, 128 * (c + 1))
        tp[span, :] = point_pieces(p_in[:, span]).T
    @pl.when(jnp.logical_and(is0, z == 0))
    def _():
        for m in range(1, 4):
            m3_from(m).wait_recv()
        owner = lax.div(x, 2) * 2 + 1
        xpath[0] = xpiece[owner, 1]
        xpath[1] = xpiece[2, 1]
        xpath[2] = xpiece[owner, 2 * lax.rem(x, 2)]
        for m in FAR_FIRST:
            mx(m).start()

    permute(tp, gp, 0, PTS // 2)

    @pl.when(is0)
    def _():
        for m in range(1, 8):
            mw_from(m).wait_recv()
        for i in range(3):
            wlev[y, i] = wpiece[lax.div(z, 2 << i) * (2 << i) + (1 << i)]
        for m in FAR_FIRST:
            m4w(m).start()

    permute(tp, gp, PTS // 2, PTS)

    for t in range(LEAVES):
        pts[t] = gp[pl.ds(starts[t], LEAF), :].astype(BF16)

    eye = (
        lax.broadcasted_iota(jnp.int32, (LEAF, LEAF), 0) == lax.broadcasted_iota(jnp.int32, (LEAF, LEAF), 1)
    ).astype(F32)
    shift = (
        lax.broadcasted_iota(jnp.int32, (R, R), 0) == lax.broadcasted_iota(jnp.int32, (R, R), 1) + 64
    ).astype(F32).astype(BF16)

    def nearby(t, carry):
        left = pts[t]
        right = dot(left, shift).astype(BF16)
        kernel = (jnp.exp(dot(left, right, 1, 1)) + eye).astype(BF16)
        near[t] = dot(kernel, rows[t])
        return carry

    lax.fori_loop(0, 4, nearby, 0, unroll=4)

    @pl.when(is0)
    def _():
        for m in range(1, 8):
            m2_from(m).wait_recv()

        @pl.when(z > 0)
        def _():
            mx(1).wait_recv()

        for i in range(3):
            xlev[y, i] = piece[lax.div(z, 2 << i) * (2 << i) + (1 << i), 1]
        xlev[y, 3:6] = xpath[...]
        for m in FAR_FIRST:
            m5(m).start()

    @pl.when(is0)
    def _():
        for m in range(1, 8):
            m4w_from(m).wait_recv()
        for i in range(3):
            mat_w[3 + i] = wlev[:, i].reshape(R, R).astype(BF16)
        for m in range(1, 8):
            ys(m).wait_recv()
        u = yslice[0]
        for m in range(1, 8):
            u = u + yslice[m]
        for i in range(3):
            zsend[i, 0] = u
            u = mm(u, mat_w[3 + i])
        for i in range(3):
            zsend[i, 1] = u
        for m in FAR_FIRST:
            zs(m).start()
        for m in FAR_FIRST:
            yb(m).start()

    lax.fori_loop(4, LEAVES, nearby, 0, unroll=4)

    @pl.when(is0)
    def _():
        for m in range(1, 8):
            m5_from(m).wait_recv()
        mat_w[6] = xlev[:, 5].reshape(R, R).astype(BF16)

        for m in range(1, 8):
            zs(m).wait_recv()
        u = zsend[0, 1]
        for m in range(1, 8):
            u = u + zgot[m, 1]
        xsend[0] = u
        xsend[1] = mm(u, mat_w[6])
        for m in (2, 3, 1):
            xs(m).start()
        sides = [lax.rem(lax.div(z, 1 << i), 2) for i in range(3)] + [lax.rem(x, 2), lax.div(x, 2)]
        for i in range(5):
            c = xlev[:, i].reshape(R, R)
            mat_c[3 + i] = jnp.where(sides[i] == 0, c.T, c).astype(BF16)
        side_z = [
            mm(zgot[1, 0], mat_c[3]),
            mm(zgot[2, 0] + zgot[3, 0], mat_c[4]),
            mm((zgot[4, 0] + zgot[5, 0]) + (zgot[6, 0] + zgot[7, 0]), mat_c[5]),
        ]
        z_path = mm(dot(mat_w[3], mat_w[4]), mat_w[5])
        x_path = mm(z_path, mat_w[6])
        far[0:R] = exact_mmt(mat_c[7], x_path)
        far[R:] = exact_mmt(mat_c[6], z_path)
        before = mmt(mmt(side_z[2], mat_w[4]) + side_z[1], mat_w[3]) + side_z[0]
        for m in range(1, 4):
            xs(m).wait_recv()
        g = mm3(jnp.concatenate([xgot[2] + xgot[3], xgot[1]], axis=1), far[...]) + before
        gdown[...] = g
        for m in FAR_FIRST:
            yd(m).start()
        fdown[y] = g

        wait_path(1)
        for level in range(3):
            c = path[level, 1]
            mat_c[level] = jnp.where(lax.rem(lax.div(y, 1 << level), 2) == 0, c.T, c).astype(BF16)
        for m in range(1, 8):
            yb(m).wait_recv()
        side_y = [
            mm(yblock[1], mat_c[0]),
            mm(yblock[2] + yblock[3], mat_c[1]),
            mm((yblock[4] + yblock[5]) + (yblock[6] + yblock[7]), mat_c[2]),
        ]
        pair = jnp.concatenate([core_mats[0], core_mats[2]], axis=0).astype(BF16)
        between = core_mats[1].astype(BF16)
        y_path = mm(dot(mat_w[0], mat_w[1]), mat_w[2])
        far[...] = exact_mm(pair, y_path)
        before = mmt(mmt(mmt(side_y[2], mat_w[1]) + side_y[1], mat_w[0]) + side_y[0], pair)
        first = before[:, :R] + mmt(core_coef[...], between)
        second = before[:, R:] + mm(coef[30], between)
        for m in range(1, 8):
            yd_from(m).wait_recv()
        both = mmt3(fdown[...].reshape(R, R), far[...])
        up_field[...] = both[:, R:] + second
        field[30] = both[:, :R] + first
        c_field().start()

    @pl.when(is1)
    def _():
        c_field().wait_recv()

    for j in range(14, -1, -1):
        both = mmt(field[16 + j], transfer[j])
        field[2 * j] = both[:, :R] + term[2 * j]
        field[2 * j + 1] = both[:, R:] + term[2 * j + 1]

    for t in range(LEAVES):
        total[t] = (near[t] + dot(basis[t], field[t].astype(BF16), 1, 1)).astype(BF16)

    @pl.when(is1)
    def _():
        c_mats().wait_send()

    @pl.when(is0)
    def _():
        c_field().wait_send()

        @pl.when(y == 0)
        def _():
            for k in range(1, 8):
                m1(k).wait_send()

        for level in range(3):
            size = 2 << level

            @pl.when(lax.rem(y, size) == size // 2)
            def _():
                for c in direct_all(level, 0) + direct_all(level, 1):
                    c.wait_send()

        for m in range(1, 8):
            for group in (mw, m4w, m2, m5, ys, yb, zs, yd):
                group(m).wait_send()
        for m in range(1, 4):
            xs(m).wait_send()

        @pl.when(z == 0)
        def _():
            for m in range(1, 4):
                m3(m).wait_send()
            for m in range(1, 8):
                mx(m).wait_send()


def tree(order, sizes, values, points, basis, transfer, coupling, ctrans, ccoup):
    dma = pltpu.SemaphoreType.DMA
    block = (R, R)
    return pl.pallas_call(
        tree_kernel,
        out_shape=jax.ShapeDtypeStruct((LEAVES, LEAF, R), BF16),
        in_specs=[SMEM, SMEM, HBM, HBM, HBM, HBM, HBM, VMEM, VMEM],
        out_specs=VMEM,
        scratch_shapes=[
            pltpu.VMEM((PTS, R), BF16),
            pltpu.VMEM((8, PTS), F32),
            pltpu.VMEM((LEAVES, LEAF, R), BF16),
            pltpu.VMEM((LEAVES - 1, 2 * R, R), BF16),
            pltpu.VMEM((LEAVES - 1,) + block, BF16),
            dma((5,)),
            pltpu.VMEM((PTS, R), F32),
            pltpu.VMEM((PTS, R), F32),
            pltpu.VMEM((PTS + LEAF, R), F32),
            pltpu.VMEM((PTS + LEAF, R), F32),
            pltpu.VMEM((LEAVES, LEAF, R), BF16),
            pltpu.VMEM((LEAVES, LEAF, R), BF16),
            pltpu.VMEM((31,) + block, F32),
            pltpu.VMEM((30,) + block, F32),
            pltpu.VMEM((31,) + block, F32),
            pltpu.VMEM((LEAVES, LEAF, R), F32),
            pltpu.VMEM((3,) + block, F32),
            pltpu.VMEM((3,) + block, F32),
            pltpu.VMEM(block, F32),
            pltpu.VMEM(block, F32),
            pltpu.VMEM((3, 2) + block, F32),
            pltpu.VMEM((8, 3, 16, R), F32),
            pltpu.VMEM((8, 16, R), F32),
            pltpu.VMEM((8, 3, 16, R), F32),
            pltpu.VMEM((4, 3, 16, R), F32),
            pltpu.VMEM((3, 16, R), F32),
            pltpu.VMEM((8, 6, 16, R), F32),
            pltpu.VMEM((7,) + block, BF16),
            pltpu.VMEM((8,) + block, BF16),
            pltpu.VMEM((2 * R, R), F32),
            pltpu.VMEM((4,) + block, F32),
            pltpu.VMEM((8, 16, R), F32),
            pltpu.VMEM((8,) + block, F32),
            pltpu.VMEM((3, 2, 16, R), F32),
            pltpu.VMEM((8, 2, 16, R), F32),
            pltpu.VMEM((2, 16, R), F32),
            pltpu.VMEM((4, 16, R), F32),
            pltpu.VMEM((16, R), F32),
            pltpu.VMEM((8, 16, R), F32),
            dma((3,)), dma((3,)),
            dma((2, 8)), dma((2, 3)),
            dma((8,)), dma,
            dma((8,)), dma((8,)),
            dma((8,)), dma((8,)),
            dma((8,)), dma((8,)),
            dma((4,)), dma((4,)),
            dma((8,)), dma,
            dma((8,)), dma((8,)),
            dma((8,)), dma((8,)),
            dma((8,)), dma((8,)),
            dma((8,)), dma((8,)),
            dma((4,)), dma((4,)),
            dma((8,)), dma((8,)),
        ],
        compiler_params=pltpu.CompilerParams(
            collective_id=0, has_side_effects=True, vmem_limit_bytes=VMEM_LIMIT
        ),
        name="tree",
    )(order, sizes, values, points, basis, transfer, coupling, ctrans, ccoup)


def body(
    values,
    points,
    tree_order,
    leaf_sizes,
    leaf_basis,
    local_transfer,
    local_coupling,
    cross_transfer,
    cross_coupling,
):
    transfer = local_transfer.reshape(LEAVES - 1, 2 * R, R)
    total = tree(
        tree_order, leaf_sizes, values, points,
        leaf_basis, transfer, local_coupling, cross_transfer, cross_coupling,
    )
    return scatter(total, tree_order, leaf_sizes)


def solution(mesh):
    in_specs = (
        P("leaf", None),
        P(None, "leaf"),
        P("leaf", None),
        P("leaf", None),
        P("leaf", None, None),
        P("leaf", None, None, None),
        P("leaf", None, None),
        P("leaf", None, None, None),
        P("leaf", None, None),
    )
    out_specs = P("leaf", None)
    return jax.shard_map(body, mesh=mesh, in_specs=in_specs, out_specs=out_specs, check_vma=False)
```

```python
import functools

import jax
import jax.numpy as jnp
from jax import lax
from jax.experimental import pallas as pl
from jax.experimental.pallas import tpu as pltpu
from jax.sharding import PartitionSpec as P

F32 = jnp.float32
BF16 = jnp.bfloat16
MESH = pl.DeviceIdType.MESH
VMEM = pl.BlockSpec(memory_space=pltpu.VMEM)
SMEM = pl.BlockSpec(memory_space=pltpu.SMEM)
HBM = pl.BlockSpec(memory_space=pl.ANY)
VMEM_LIMIT = 56 * 2**20

PTS = 3072
LEAF = 256
LEAVES = 16
R = 128
UNROLL = 128
FAR_FIRST = (4, 5, 3, 7, 6, 2, 1)


def point_pieces(p):
    h = p.astype(BF16).astype(F32)
    rest = p - h
    m = rest.astype(BF16).astype(F32)
    low = (rest - m).astype(BF16).astype(F32)
    q = jnp.sum(p * p, axis=0, keepdims=True) * -0.125
    qh = q.astype(BF16).astype(F32)
    rest = q - qh
    qm = rest.astype(BF16).astype(F32)
    ql = (rest - qm).astype(BF16).astype(F32)
    n = p.shape[1]
    row = lax.broadcasted_iota(jnp.int32, (8, n), 0)
    parts = jnp.where(row % 3 == 0, qh, jnp.where(row % 3 == 1, qm, ql))
    left_q = jnp.where(row < 3, parts, jnp.where(row < 6, 1.0, 0.0))
    right_q = jnp.where(row < 3, 1.0, jnp.where(row < 6, parts, 0.0))
    zero = jnp.zeros((8, n), F32)
    left = [h * 0.25, h * 0.25, m * 0.25, m * 0.25, h * 0.25, low * 0.25, left_q, zero]
    right = [h, m, h, m, low, h, right_q, zero]
    return jnp.concatenate(left + right, axis=0)


def scatter_kernel(order, sizes, total, out, tree, held):
    start = 0
    for t in range(LEAVES):
        tree[pl.ds(start, LEAF), :] = total[t].astype(F32)
        start = start + sizes[0, t]

    def move(i, carry):
        base = pl.multiple_of(i * UNROLL, UNROLL)
        for u in range(UNROLL):
            held[pl.ds(order[0, base + u], 1), :] = tree[pl.ds(base + u, 1), :]
        return carry

    lax.fori_loop(0, PTS // UNROLL, move, 0)
    out[...] = held[...].astype(BF16)


def scatter(total, order, sizes):
    return pl.pallas_call(
        scatter_kernel,
        out_shape=jax.ShapeDtypeStruct((PTS, R), BF16),
        in_specs=[SMEM, SMEM, VMEM],
        out_specs=VMEM,
        scratch_shapes=[
            pltpu.VMEM((PTS + LEAF, R), F32),
            pltpu.VMEM((PTS, R), F32),
        ],
        compiler_params=pltpu.CompilerParams(vmem_limit_bytes=56 * 2**20),
        name="scatter_rows",
    )(order, sizes, total)


def dot(a, b, ca=1, cb=0):
    return lax.dot_general(a, b, (((ca,), (cb,)), ((), ())), preferred_element_type=F32)


def split(x):
    h = x.astype(BF16)
    return jnp.concatenate([h, (x - h.astype(F32)).astype(BF16)], axis=0)


def mm(x, w):
    y = dot(split(x), w)
    return y[: x.shape[0]] + y[x.shape[0] :]


def mmt(x, w):
    y = dot(split(x), w, 1, 1)
    return y[: x.shape[0]] + y[x.shape[0] :]


def mmt3(x, w):
    h = w.astype(BF16)
    return mmt(x, h) + dot(x.astype(BF16), (w - h.astype(F32)).astype(BF16), 1, 1)


def mm3(x, w):
    h = w.astype(BF16)
    return mm(x, h) + dot(x.astype(BF16), (w - h.astype(F32)).astype(BF16))


def exact_mmt(x, w):
    h = w.astype(BF16)
    return dot(x, h, 1, 1) + dot(x, (w - h.astype(F32)).astype(BF16), 1, 1)


def exact_mm(x, w):
    h = w.astype(BF16)
    return dot(x, h) + dot(x, (w - h.astype(F32)).astype(BF16))


def flip(v, m):
    out = v
    for i in range(3):
        if (m >> i) & 1:
            bit = lax.rem(lax.div(v, 2**i), 2)
            out = out + (1 - 2 * bit) * 2**i
    return out


def reach(m):
    return m.bit_length() - 1


def tree_kernel(
    order, sizes, v_ref, p_ref, basis_any, transfer_any, coupling_any, ctrans, ccoup, total,
    v_in, p_in, basis, transfer, coupling, s_local, tv, tp, gv, gp, rows, pts,
    coef, term, field, near, own, core_mats, core_coef, up_field,
    path, piece, wpiece, wlev, xpiece, xpath, w8lev, xlev, mat_w, mat_c,
    far, prod, yslice, yblock, zsend, zgot, xsend, xgot, gdown, fdown,
    s_core, r_core, s_dir, r_dir, s_m1, r_m1, s_mw, r_mw, s_m4w, r_m4w, s_m2, r_m2, s_m3, r_m3, s_mx, r_mx, s_m5, r_m5, s_m6, r_m6,
    s_ys, r_ys, s_yb, r_yb, s_z, r_z, s_x, r_x, s_yd, r_yd,
):
    me = lax.axis_index("leaf")
    core = lax.rem(me, 2)
    y = lax.rem(lax.div(me, 2), 8)
    z = lax.rem(lax.div(me, 16), 8)
    x = lax.div(me, 128)
    is0 = core == 0
    is1 = core == 1

    def at(xx, zz, yy):
        return ((xx * 8 + zz) * 8 + yy) * 2

    mate = me + 1 - 2 * core
    along_y = [at(x, z, flip(y, m)) for m in range(8)]
    along_z = [at(x, flip(z, m), y) for m in range(8)]
    along_x = [at(flip(x, m), z, y) for m in range(4)]

    def copy(src, dst, send, recv, to):
        return pltpu.make_async_remote_copy(
            src_ref=src, dst_ref=dst, send_sem=send, recv_sem=recv, device_id=(to,), device_id_type=MESH
        )

    barrier = pltpu.get_barrier_semaphore()
    pl.semaphore_signal(barrier, inc=1, device_id=(mate,), device_id_type=MESH)

    @pl.when(is0)
    def _():
        partners = [line[m] for m in FAR_FIRST for line in (along_y, along_z)]
        for to in partners + along_x[1:]:
            pl.semaphore_signal(barrier, inc=1, device_id=(to,), device_id_type=MESH)

    loads = [
        pltpu.make_async_copy(src, dst, s_local.at[i])
        for i, (src, dst) in enumerate(
            [(v_ref, v_in), (p_ref, p_in), (basis_any, basis), (transfer_any, transfer), (coupling_any, coupling)]
        )
    ]
    for load in loads:
        load.start()

    own[0] = ctrans[0, 0].astype(F32)
    own[1] = ctrans[0, 1].astype(F32)
    own[2] = ccoup[0].astype(F32)

    loads[0].wait()
    tv[...] = v_in[...].astype(F32)
    gv[PTS:, :] = jnp.zeros((LEAF, R), F32)
    gp[PTS:, :] = jnp.zeros((LEAF, R), F32)

    @pl.when(is0)
    def _():
        pl.semaphore_wait(barrier, 18)

    @pl.when(is1)
    def _():
        pl.semaphore_wait(barrier, 1)

    def c_mats():
        return copy(own, core_mats, s_core.at[0], r_core.at[0], mate)

    def c_coef():
        return copy(coef.at[30], core_coef, s_core.at[1], r_core.at[1], mate)

    def c_field():
        return copy(up_field, field.at[30], s_core.at[2], r_core.at[2], mate)


    def direct(level, i, which):
        size = 2 << level
        half = size // 2
        src = own.at[2] if which else own.at[0 if i < half else 1]
        to = at(x, z, y - half + i)
        return copy(src, path.at[level, which], s_dir.at[which, i], r_dir.at[which, level], to)

    def direct_all(level, which):
        size = 2 << level
        return [direct(level, i, which) for i in range(size) if i != size // 2]

    def m1(k, part):
        span, which = pl.ds(16 * k, 16), pl.ds(2 * part, 2 - part)
        return copy(
            own.at[which, span, :], piece.at[z, which], s_m1.at[part, k], r_m1.at[part], at(x, z, k)
        )

    def mw(m):
        to = flip(z, m)
        side = jnp.where(to < z, 0, 1)
        return copy(piece.at[z, side], wpiece.at[z], s_mw.at[m], r_mw.at[m], along_z[m])

    def mw_from(m):
        return copy(piece.at[z, 0], wpiece.at[flip(z, m)], s_mw.at[m], r_mw.at[m], along_z[m])

    def m4w(m):
        return copy(wlev.at[y], wlev.at[y], s_m4w.at[m], r_m4w.at[m], along_y[m])

    def m4w_from(m):
        return copy(wlev.at[y], wlev.at[flip(y, m)], s_m4w.at[m], r_m4w.at[m], along_y[m])

    def m2(m):
        return copy(piece.at[z, 2], piece.at[z, 2], s_m2.at[m], r_m2.at[m], along_z[m])

    def m2_from(m):
        there = piece.at[flip(z, m), 2]
        return copy(there, there, s_m2.at[m], r_m2.at[m], along_z[m])

    def m3(m):
        return copy(piece.at[0], xpiece.at[x], s_m3.at[m], r_m3.at[m], along_x[m])

    def mx(m):
        return copy(xpath, xpath, s_mx.at[m], r_mx, at(x, m, y))

    def m3_from(m):
        return copy(piece.at[0], xpiece.at[flip(x, m)], s_m3.at[m], r_m3.at[m], along_x[m])

    def m5(m):
        return copy(xlev.at[y], xlev.at[y], s_m5.at[m], r_m5.at[m], along_y[m])

    def m5_from(m):
        return copy(xlev.at[y], xlev.at[flip(y, m)], s_m5.at[m], r_m5.at[m], along_y[m])

    def m6(m):
        return copy(w8lev.at[y], w8lev.at[y], s_m6.at[m], r_m6.at[m], along_y[m])

    def m6_from(m):
        return copy(w8lev.at[y], w8lev.at[flip(y, m)], s_m6.at[m], r_m6.at[m], along_y[m])

    def ys(m):
        part = prod.at[3, pl.ds(pl.multiple_of(16 * flip(y, m), 16), 16), :]
        return copy(part, yslice.at[m], s_ys.at[m], r_ys.at[m], along_y[m])

    def yb(m):
        return copy(prod.at[reach(m)], yblock.at[m], s_yb.at[m], r_yb.at[m], along_y[m])

    def zs(m):
        return copy(zsend.at[reach(m)], zgot.at[m], s_z.at[m], r_z.at[m], along_z[m])

    def xs(m):
        return copy(xsend.at[reach(m)], xgot.at[m], s_x.at[m], r_x.at[m], along_x[m])

    def yd(m):
        return copy(gdown, fdown.at[y], s_yd.at[m], r_yd.at[m], along_y[m])

    def yd_from(m):
        return copy(gdown, fdown.at[flip(y, m)], s_yd.at[m], r_yd.at[m], along_y[m])

    @pl.when(is1)
    def _():
        c_mats().start()

    @pl.when(is0)
    def _():
        @pl.when(y == 0)
        def _():
            for k in (4, 3, 5, 2, 6, 1, 7):
                m1(k, 0).start()
            for k in (4, 3, 5, 2, 6, 1, 7):
                m1(k, 1).start()
            piece[z] = own[:, 0:16, :]

        for level in (2,):
            size = 2 << level

            @pl.when(lax.rem(y, size) == size // 2)
            def _():
                for c in direct_all(level, 0):
                    c.start()
                path[level, 0] = own[1]
                path[level, 1] = own[2]

    def wait_path(which):
        for level in range(3):
            size = 2 << level

            @pl.when(lax.rem(y, size) != size // 2)
            def _():
                got = path.at[level, which]
                copy(own.at[0], got, s_dir.at[0, 0], r_dir.at[which, level], mate).wait_recv()

    def permute(table, placed, first, last):
        def move(i, carry):
            base = pl.multiple_of(i * UNROLL, UNROLL)
            for u in range(UNROLL):
                placed[pl.ds(base + u, 1), :] = table[pl.ds(order[0, base + u], 1), :]
            return carry

        lax.fori_loop(first // UNROLL, last // UNROLL, move, 0)

    permute(tv, gv, 0, PTS)

    @pl.when(is0)
    def _():
        for level in (1, 0):
            size = 2 << level

            @pl.when(lax.rem(y, size) == size // 2)
            def _():
                for c in direct_all(level, 0):
                    c.start()
                path[level, 0] = own[1]
                path[level, 1] = own[2]


    slot = lax.broadcasted_iota(jnp.int32, (LEAF, R), 0)
    starts = [0]
    for t in range(LEAVES):
        size = sizes[0, t]
        rows[t] = jnp.where(slot < size, gv[pl.ds(starts[t], LEAF), :], 0.0).astype(BF16)
        starts.append(starts[t] + size)
    loads[2].wait()
    for t in range(LEAVES):
        coef[t] = dot(rows[t], basis[t], 0, 0)
    loads[3].wait()
    for j in range(15):
        both = jnp.concatenate([coef[2 * j], coef[2 * j + 1]], axis=1)
        coef[16 + j] = mm(both, transfer[j])
    c_coef().start()

    @pl.when(is0)
    def _():
        @pl.when(y > 0)
        def _():
            m1(1, 0).wait_recv()

        for m in FAR_FIRST:
            mw(m).start()
        wpiece[z] = piece[z, 1]

        @pl.when(y > 0)
        def _():
            m1(1, 1).wait_recv()

        @pl.when(z == 0)
        def _():
            for m in (2, 3, 1):
                m3(m).start()
            xpiece[x] = piece[0]

        for m in FAR_FIRST:
            m2(m).start()

    loads[4].wait()
    for j in range(15):
        term[2 * j] = mmt(coef[2 * j + 1], coupling[j])
        term[2 * j + 1] = mm(coef[2 * j], coupling[j])

    @pl.when(is0)
    def _():
        wait_path(0)
        for level in range(3):
            mat_w[level] = path[level, 0].astype(BF16)
        c_mats().wait_recv()
        c_coef().wait()
        pair = jnp.concatenate([core_mats[0], core_mats[1]], axis=0).astype(BF16)
        prod[0] = mm(jnp.concatenate([coef[30], core_coef[...]], axis=1), pair)
        for level in range(3):
            prod[level + 1] = mm(prod[level], mat_w[level])
        for m in FAR_FIRST:
            ys(m).start()
        for lev in range(3):

            @pl.when(lax.rem(y, 2 << lev) == 1 << lev)
            def _():
                for c in direct_all(lev, 1):
                    c.start()

        yslice[0] = prod[3, pl.ds(pl.multiple_of(16 * y, 16), 16), :]

    @pl.when(is1)
    def _():
        c_coef().wait()

    loads[1].wait()
    for c in range(PTS // 128):
        span = slice(128 * c, 128 * (c + 1))
        tp[span, :] = point_pieces(p_in[:, span]).T
    @pl.when(jnp.logical_and(is0, z == 0))
    def _():
        for m in range(1, 4):
            m3_from(m).wait_recv()
        owner = lax.div(x, 2) * 2 + 1
        xpath[0] = xpiece[owner, 2]
        xpath[1] = xpiece[2, 2]
        xpath[2] = xpiece[owner, lax.rem(x, 2)]
        for m in FAR_FIRST:
            mx(m).start()

    @pl.when(is0)
    def _():
        for m in range(1, 8):
            mw_from(m).wait_recv()
        for i in range(3):
            wlev[y, i] = wpiece[lax.div(z, 2 << i) * (2 << i) + (1 << i)]
        for m in FAR_FIRST:
            m4w(m).start()

    permute(tp, gp, 0, PTS // 2)

    permute(tp, gp, PTS // 2, PTS)

    for t in range(LEAVES):
        pts[t] = gp[pl.ds(starts[t], LEAF), :].astype(BF16)

    eye = (
        lax.broadcasted_iota(jnp.int32, (LEAF, LEAF), 0) == lax.broadcasted_iota(jnp.int32, (LEAF, LEAF), 1)
    ).astype(F32)
    shift = (
        lax.broadcasted_iota(jnp.int32, (R, R), 0) == lax.broadcasted_iota(jnp.int32, (R, R), 1) + 64
    ).astype(F32).astype(BF16)

    def nearby(t, carry):
        left = pts[t]
        right = dot(left, shift).astype(BF16)
        kernel = (jnp.exp(dot(left, right, 1, 1)) + eye).astype(BF16)
        near[t] = dot(kernel, rows[t])
        return carry

    lax.fori_loop(0, 4, nearby, 0, unroll=4)

    @pl.when(is0)
    def _():
        @pl.when(z > 0)
        def _():
            mx(1).wait_recv()

        w8lev[y] = xpath[2]
        for m in FAR_FIRST:
            m6(m).start()
        for m in range(1, 8):
            m2_from(m).wait_recv()
        for i in range(3):
            xlev[y, i] = piece[lax.div(z, 2 << i) * (2 << i) + (1 << i), 2]
        xlev[y, 3:5] = xpath[0:2]
        for m in FAR_FIRST:
            m5(m).start()

    @pl.when(is0)
    def _():
        for m in range(1, 8):
            m4w_from(m).wait_recv()
        for i in range(3):
            mat_w[3 + i] = wlev[:, i].reshape(R, R).astype(BF16)
        for m in range(1, 8):
            ys(m).wait_recv()
        u = yslice[0]
        for m in range(1, 8):
            u = u + yslice[m]
        for i in range(3):
            zsend[i, 0] = u
            u = mm(u, mat_w[3 + i])
        for i in range(3):
            zsend[i, 1] = u
        for m in FAR_FIRST:
            zs(m).start()
        for m in FAR_FIRST:
            yb(m).start()

    lax.fori_loop(4, 12, nearby, 0, unroll=8)

    @pl.when(is0)
    def _():
        for m in range(1, 8):
            m6_from(m).wait_recv()
        mat_w[6] = w8lev[...].reshape(R, R).astype(BF16)

        for m in range(1, 8):
            zs(m).wait_recv()
        u = zsend[0, 1]
        for m in range(1, 8):
            u = u + zgot[m, 1]
        xsend[0] = u
        xsend[1] = mm(u, mat_w[6])
        for m in (2, 3, 1):
            xs(m).start()

    lax.fori_loop(12, LEAVES, nearby, 0, unroll=4)

    @pl.when(is0)
    def _():
        for m in range(1, 8):
            m5_from(m).wait_recv()
        sides = [lax.rem(lax.div(z, 1 << i), 2) for i in range(3)] + [lax.rem(x, 2), lax.div(x, 2)]
        for i in range(5):
            c = xlev[:, i].reshape(R, R)
            mat_c[3 + i] = jnp.where(sides[i] == 0, c.T, c).astype(BF16)
        side_z = [
            mm(zgot[1, 0], mat_c[3]),
            mm(zgot[2, 0] + zgot[3, 0], mat_c[4]),
            mm((zgot[4, 0] + zgot[5, 0]) + (zgot[6, 0] + zgot[7, 0]), mat_c[5]),
        ]
        z_path = mm(dot(mat_w[3], mat_w[4]), mat_w[5])
        x_path = mm(z_path, mat_w[6])
        far[0:R] = exact_mmt(mat_c[7], x_path)
        far[R:] = exact_mmt(mat_c[6], z_path)
        before = mmt(mmt(side_z[2], mat_w[4]) + side_z[1], mat_w[3]) + side_z[0]
        for m in range(1, 4):
            xs(m).wait_recv()
        g = mm3(jnp.concatenate([xgot[2] + xgot[3], xgot[1]], axis=1), far[...]) + before
        gdown[...] = g
        for m in FAR_FIRST:
            yd(m).start()
        fdown[y] = g

        wait_path(1)
        for level in range(3):
            c = path[level, 1]
            mat_c[level] = jnp.where(lax.rem(lax.div(y, 1 << level), 2) == 0, c.T, c).astype(BF16)
        for m in range(1, 8):
            yb(m).wait_recv()
        side_y = [
            mm(yblock[1], mat_c[0]),
            mm(yblock[2] + yblock[3], mat_c[1]),
            mm((yblock[4] + yblock[5]) + (yblock[6] + yblock[7]), mat_c[2]),
        ]
        pair = jnp.concatenate([core_mats[0], core_mats[1]], axis=0).astype(BF16)
        between = core_mats[2].astype(BF16)
        y_path = mm(dot(mat_w[0], mat_w[1]), mat_w[2])
        far[...] = exact_mm(pair, y_path)
        before = mmt(mmt(mmt(side_y[2], mat_w[1]) + side_y[1], mat_w[0]) + side_y[0], pair)
        first = before[:, :R] + mmt(core_coef[...], between)
        second = before[:, R:] + mm(coef[30], between)
        for m in range(1, 8):
            yd_from(m).wait_recv()
        both = mmt3(fdown[...].reshape(R, R), far[...])
        up_field[...] = both[:, R:] + second
        field[30] = both[:, :R] + first
        c_field().start()

    @pl.when(is1)
    def _():
        c_field().wait_recv()

    for j in range(14, -1, -1):
        both = mmt(field[16 + j], transfer[j])
        field[2 * j] = both[:, :R] + term[2 * j]
        field[2 * j + 1] = both[:, R:] + term[2 * j + 1]

    for t in range(LEAVES):
        total[t] = (near[t] + dot(basis[t], field[t].astype(BF16), 1, 1)).astype(BF16)

    @pl.when(is1)
    def _():
        c_mats().wait_send()

    @pl.when(is0)
    def _():
        c_field().wait_send()

        @pl.when(y == 0)
        def _():
            for k in range(1, 8):
                m1(k, 0).wait_send()
                m1(k, 1).wait_send()

        for level in range(3):
            size = 2 << level

            @pl.when(lax.rem(y, size) == size // 2)
            def _():
                for c in direct_all(level, 0) + direct_all(level, 1):
                    c.wait_send()

        for m in range(1, 8):
            for group in (mw, m4w, m2, m5, m6, ys, yb, zs, yd):
                group(m).wait_send()
        for m in range(1, 4):
            xs(m).wait_send()

        @pl.when(z == 0)
        def _():
            for m in range(1, 4):
                m3(m).wait_send()
            for m in range(1, 8):
                mx(m).wait_send()


def tree(order, sizes, values, points, basis, transfer, coupling, ctrans, ccoup):
    dma = pltpu.SemaphoreType.DMA
    block = (R, R)
    return pl.pallas_call(
        tree_kernel,
        out_shape=jax.ShapeDtypeStruct((LEAVES, LEAF, R), BF16),
        in_specs=[SMEM, SMEM, HBM, HBM, HBM, HBM, HBM, VMEM, VMEM],
        out_specs=VMEM,
        scratch_shapes=[
            pltpu.VMEM((PTS, R), BF16),
            pltpu.VMEM((8, PTS), F32),
            pltpu.VMEM((LEAVES, LEAF, R), BF16),
            pltpu.VMEM((LEAVES - 1, 2 * R, R), BF16),
            pltpu.VMEM((LEAVES - 1,) + block, BF16),
            dma((5,)),
            pltpu.VMEM((PTS, R), F32),
            pltpu.VMEM((PTS, R), F32),
            pltpu.VMEM((PTS + LEAF, R), F32),
            pltpu.VMEM((PTS + LEAF, R), F32),
            pltpu.VMEM((LEAVES, LEAF, R), BF16),
            pltpu.VMEM((LEAVES, LEAF, R), BF16),
            pltpu.VMEM((31,) + block, F32),
            pltpu.VMEM((30,) + block, F32),
            pltpu.VMEM((31,) + block, F32),
            pltpu.VMEM((LEAVES, LEAF, R), F32),
            pltpu.VMEM((3,) + block, F32),
            pltpu.VMEM((3,) + block, F32),
            pltpu.VMEM(block, F32),
            pltpu.VMEM(block, F32),
            pltpu.VMEM((3, 2) + block, F32),
            pltpu.VMEM((8, 3, 16, R), F32),
            pltpu.VMEM((8, 16, R), F32),
            pltpu.VMEM((8, 3, 16, R), F32),
            pltpu.VMEM((4, 3, 16, R), F32),
            pltpu.VMEM((3, 16, R), F32),
            pltpu.VMEM((8, 16, R), F32),
            pltpu.VMEM((8, 5, 16, R), F32),
            pltpu.VMEM((7,) + block, BF16),
            pltpu.VMEM((8,) + block, BF16),
            pltpu.VMEM((2 * R, R), F32),
            pltpu.VMEM((4,) + block, F32),
            pltpu.VMEM((8, 16, R), F32),
            pltpu.VMEM((8,) + block, F32),
            pltpu.VMEM((3, 2, 16, R), F32),
            pltpu.VMEM((8, 2, 16, R), F32),
            pltpu.VMEM((2, 16, R), F32),
            pltpu.VMEM((4, 16, R), F32),
            pltpu.VMEM((16, R), F32),
            pltpu.VMEM((8, 16, R), F32),
            dma((3,)), dma((3,)),
            dma((2, 8)), dma((2, 3)),
            dma((2, 8)), dma((2,)),
            dma((8,)), dma((8,)),
            dma((8,)), dma((8,)),
            dma((8,)), dma((8,)),
            dma((4,)), dma((4,)),
            dma((8,)), dma,
            dma((8,)), dma((8,)),
            dma((8,)), dma((8,)),
            dma((8,)), dma((8,)),
            dma((8,)), dma((8,)),
            dma((8,)), dma((8,)),
            dma((4,)), dma((4,)),
            dma((8,)), dma((8,)),
        ],
        compiler_params=pltpu.CompilerParams(
            collective_id=0, has_side_effects=True, vmem_limit_bytes=VMEM_LIMIT
        ),
        name="tree",
    )(order, sizes, values, points, basis, transfer, coupling, ctrans, ccoup)


def body(
    values,
    points,
    tree_order,
    leaf_sizes,
    leaf_basis,
    local_transfer,
    local_coupling,
    cross_transfer,
    cross_coupling,
):
    transfer = local_transfer.reshape(LEAVES - 1, 2 * R, R)
    total = tree(
        tree_order, leaf_sizes, values, points,
        leaf_basis, transfer, local_coupling, cross_transfer, cross_coupling,
    )
    return scatter(total, tree_order, leaf_sizes)


def solution(mesh):
    in_specs = (
        P("leaf", None),
        P(None, "leaf"),
        P("leaf", None),
        P("leaf", None),
        P("leaf", None, None),
        P("leaf", None, None, None),
        P("leaf", None, None),
        P("leaf", None, None, None),
        P("leaf", None, None),
    )
    out_specs = P("leaf", None)
    return jax.shard_map(body, mesh=mesh, in_specs=in_specs, out_specs=out_specs, check_vma=False)
```

```python
import functools

import jax
import jax.numpy as jnp
from jax import lax
from jax.experimental import pallas as pl
from jax.experimental.pallas import tpu as pltpu
from jax.sharding import PartitionSpec as P

F32 = jnp.float32
BF16 = jnp.bfloat16
MESH = pl.DeviceIdType.MESH
VMEM = pl.BlockSpec(memory_space=pltpu.VMEM)
SMEM = pl.BlockSpec(memory_space=pltpu.SMEM)
HBM = pl.BlockSpec(memory_space=pl.ANY)
VMEM_LIMIT = 56 * 2**20

PTS = 3072
LEAF = 256
LEAVES = 16
R = 128
UNROLL = 128
FAR_FIRST = (4, 5, 3, 7, 6, 2, 1)


def point_pieces(p):
    h = p.astype(BF16).astype(F32)
    rest = p - h
    m = rest.astype(BF16).astype(F32)
    low = (rest - m).astype(BF16).astype(F32)
    q = jnp.sum(p * p, axis=0, keepdims=True) * -0.125
    qh = q.astype(BF16).astype(F32)
    rest = q - qh
    qm = rest.astype(BF16).astype(F32)
    ql = (rest - qm).astype(BF16).astype(F32)
    n = p.shape[1]
    row = lax.broadcasted_iota(jnp.int32, (8, n), 0)
    parts = jnp.where(row % 3 == 0, qh, jnp.where(row % 3 == 1, qm, ql))
    left_q = jnp.where(row < 3, parts, jnp.where(row < 6, 1.0, 0.0))
    right_q = jnp.where(row < 3, 1.0, jnp.where(row < 6, parts, 0.0))
    zero = jnp.zeros((8, n), F32)
    left = [h * 0.25, h * 0.25, m * 0.25, m * 0.25, h * 0.25, low * 0.25, left_q, zero]
    right = [h, m, h, m, low, h, right_q, zero]
    return jnp.concatenate(left + right, axis=0)


def scatter_kernel(order, sizes, total, out, tree, held):
    start = 0
    for t in range(LEAVES):
        tree[pl.ds(start, LEAF), :] = total[t].astype(F32)
        start = start + sizes[0, t]

    def move(i, carry):
        base = pl.multiple_of(i * UNROLL, UNROLL)
        for u in range(UNROLL):
            held[pl.ds(order[0, base + u], 1), :] = tree[pl.ds(base + u, 1), :]
        return carry

    lax.fori_loop(0, PTS // UNROLL, move, 0)
    out[...] = held[...].astype(BF16)


def scatter(total, order, sizes):
    return pl.pallas_call(
        scatter_kernel,
        out_shape=jax.ShapeDtypeStruct((PTS, R), BF16),
        in_specs=[SMEM, SMEM, VMEM],
        out_specs=VMEM,
        scratch_shapes=[
            pltpu.VMEM((PTS + LEAF, R), F32),
            pltpu.VMEM((PTS, R), F32),
        ],
        compiler_params=pltpu.CompilerParams(vmem_limit_bytes=56 * 2**20),
        name="scatter_rows",
    )(order, sizes, total)


def dot(a, b, ca=1, cb=0):
    return lax.dot_general(a, b, (((ca,), (cb,)), ((), ())), preferred_element_type=F32)


def split(x):
    h = x.astype(BF16)
    return jnp.concatenate([h, (x - h.astype(F32)).astype(BF16)], axis=0)


def mm(x, w):
    y = dot(split(x), w)
    return y[: x.shape[0]] + y[x.shape[0] :]


def mmt(x, w):
    y = dot(split(x), w, 1, 1)
    return y[: x.shape[0]] + y[x.shape[0] :]


def mmt3(x, w):
    h = w.astype(BF16)
    return mmt(x, h) + dot(x.astype(BF16), (w - h.astype(F32)).astype(BF16), 1, 1)


def mm3(x, w):
    h = w.astype(BF16)
    return mm(x, h) + dot(x.astype(BF16), (w - h.astype(F32)).astype(BF16))


def exact_mmt(x, w):
    h = w.astype(BF16)
    return dot(x, h, 1, 1) + dot(x, (w - h.astype(F32)).astype(BF16), 1, 1)


def exact_mm(x, w):
    h = w.astype(BF16)
    return dot(x, h) + dot(x, (w - h.astype(F32)).astype(BF16))


def flip(v, m):
    out = v
    for i in range(3):
        if (m >> i) & 1:
            bit = lax.rem(lax.div(v, 2**i), 2)
            out = out + (1 - 2 * bit) * 2**i
    return out


def reach(m):
    return m.bit_length() - 1


def tree_kernel(
    order, sizes, v_ref, p_ref, basis_any, transfer_any, coupling_any, ctrans, ccoup, total_any,
    total, s_total, v_in, p_in, basis, transfer, coupling, s_local, tv, tp, gv, gp, rows, pts,
    coef, term, field, near, own, core_mats, core_coef, up_field,
    path, piece, wpiece, wlev, xpiece, xpath, w8lev, xlev, mat_w, mat_c,
    far, prod, yslice, yblock, zsend, zgot, xsend, xgot, gdown, fdown,
    s_core, r_core, s_dir, r_dir, s_m1, r_m1, s_mw, r_mw, s_m4w, r_m4w, s_m2, r_m2, s_m3, r_m3, s_mx, r_mx, s_m5, r_m5, s_m6, r_m6,
    s_ys, r_ys, s_yb, r_yb, s_z, r_z, s_x, r_x, s_yd, r_yd,
):
    me = lax.axis_index("leaf")
    core = lax.rem(me, 2)
    y = lax.rem(lax.div(me, 2), 8)
    z = lax.rem(lax.div(me, 16), 8)
    x = lax.div(me, 128)
    is0 = core == 0
    is1 = core == 1

    def at(xx, zz, yy):
        return ((xx * 8 + zz) * 8 + yy) * 2

    mate = me + 1 - 2 * core
    along_y = [at(x, z, flip(y, m)) for m in range(8)]
    along_z = [at(x, flip(z, m), y) for m in range(8)]
    along_x = [at(flip(x, m), z, y) for m in range(4)]

    def copy(src, dst, send, recv, to):
        return pltpu.make_async_remote_copy(
            src_ref=src, dst_ref=dst, send_sem=send, recv_sem=recv, device_id=(to,), device_id_type=MESH
        )

    barrier = pltpu.get_barrier_semaphore()
    pl.semaphore_signal(barrier, inc=1, device_id=(mate,), device_id_type=MESH)

    @pl.when(is0)
    def _():
        partners = [line[m] for m in FAR_FIRST for line in (along_y, along_z)]
        for to in partners + along_x[1:]:
            pl.semaphore_signal(barrier, inc=1, device_id=(to,), device_id_type=MESH)

    loads = [
        pltpu.make_async_copy(src, dst, s_local.at[i])
        for i, (src, dst) in enumerate(
            [(v_ref, v_in), (p_ref, p_in), (basis_any, basis), (transfer_any, transfer), (coupling_any, coupling)]
        )
    ]
    for load in loads:
        load.start()

    own[0] = ctrans[0, 0].astype(F32)
    own[1] = ctrans[0, 1].astype(F32)
    own[2] = ccoup[0].astype(F32)

    loads[0].wait()
    tv[...] = v_in[...].astype(F32)
    gv[PTS:, :] = jnp.zeros((LEAF, R), F32)
    gp[PTS:, :] = jnp.zeros((LEAF, R), F32)

    @pl.when(is0)
    def _():
        pl.semaphore_wait(barrier, 18)

    @pl.when(is1)
    def _():
        pl.semaphore_wait(barrier, 1)

    def c_mats():
        return copy(own, core_mats, s_core.at[0], r_core.at[0], mate)

    def c_coef():
        return copy(coef.at[30], core_coef, s_core.at[1], r_core.at[1], mate)

    def c_field():
        return copy(up_field, field.at[30], s_core.at[2], r_core.at[2], mate)


    def direct(level, i, which):
        size = 2 << level
        half = size // 2
        src = own.at[2] if which else own.at[0 if i < half else 1]
        to = at(x, z, y - half + i)
        return copy(src, path.at[level, which], s_dir.at[which, i], r_dir.at[which, level], to)

    def direct_all(level, which):
        size = 2 << level
        return [direct(level, i, which) for i in range(size) if i != size // 2]

    def m1(k, part):
        span, which = pl.ds(16 * k, 16), pl.ds(2 * part, 2 - part)
        return copy(
            own.at[which, span, :], piece.at[z, which], s_m1.at[part, k], r_m1.at[part], at(x, z, k)
        )

    def mw(m):
        to = flip(z, m)
        side = jnp.where(to < z, 0, 1)
        return copy(piece.at[z, side], wpiece.at[z], s_mw.at[m], r_mw.at[m], along_z[m])

    def mw_from(m):
        return copy(piece.at[z, 0], wpiece.at[flip(z, m)], s_mw.at[m], r_mw.at[m], along_z[m])

    def m4w(m):
        return copy(wlev.at[y], wlev.at[y], s_m4w.at[m], r_m4w.at[m], along_y[m])

    def m4w_from(m):
        return copy(wlev.at[y], wlev.at[flip(y, m)], s_m4w.at[m], r_m4w.at[m], along_y[m])

    def m2(m):
        return copy(piece.at[z, 2], piece.at[z, 2], s_m2.at[m], r_m2.at[m], along_z[m])

    def m2_from(m):
        there = piece.at[flip(z, m), 2]
        return copy(there, there, s_m2.at[m], r_m2.at[m], along_z[m])

    def m3(m):
        return copy(piece.at[0], xpiece.at[x], s_m3.at[m], r_m3.at[m], along_x[m])

    def mx(m):
        return copy(xpath, xpath, s_mx.at[m], r_mx, at(x, m, y))

    def m3_from(m):
        return copy(piece.at[0], xpiece.at[flip(x, m)], s_m3.at[m], r_m3.at[m], along_x[m])

    def m5(m):
        return copy(xlev.at[y], xlev.at[y], s_m5.at[m], r_m5.at[m], along_y[m])

    def m5_from(m):
        return copy(xlev.at[y], xlev.at[flip(y, m)], s_m5.at[m], r_m5.at[m], along_y[m])

    def m6(m):
        return copy(w8lev.at[y], w8lev.at[y], s_m6.at[m], r_m6.at[m], along_y[m])

    def m6_from(m):
        return copy(w8lev.at[y], w8lev.at[flip(y, m)], s_m6.at[m], r_m6.at[m], along_y[m])

    def ys(m):
        part = prod.at[3, pl.ds(pl.multiple_of(16 * flip(y, m), 16), 16), :]
        return copy(part, yslice.at[m], s_ys.at[m], r_ys.at[m], along_y[m])

    def yb(m):
        return copy(prod.at[reach(m)], yblock.at[m], s_yb.at[m], r_yb.at[m], along_y[m])

    def zs(m):
        return copy(zsend.at[reach(m)], zgot.at[m], s_z.at[m], r_z.at[m], along_z[m])

    def xs(m):
        return copy(xsend.at[reach(m)], xgot.at[m], s_x.at[m], r_x.at[m], along_x[m])

    def yd(m):
        return copy(gdown, fdown.at[y], s_yd.at[m], r_yd.at[m], along_y[m])

    def yd_from(m):
        return copy(gdown, fdown.at[flip(y, m)], s_yd.at[m], r_yd.at[m], along_y[m])

    @pl.when(is1)
    def _():
        c_mats().start()

    @pl.when(is0)
    def _():
        @pl.when(y == 0)
        def _():
            for k in (4, 3, 5, 2, 6, 1, 7):
                m1(k, 0).start()
            for k in (4, 3, 5, 2, 6, 1, 7):
                m1(k, 1).start()
            piece[z] = own[:, 0:16, :]

        for level in range(3):
            size = 2 << level

            @pl.when(lax.rem(y, size) == size // 2)
            def _():
                for c in direct_all(level, 0):
                    c.start()
                path[level, 0] = own[1]
                path[level, 1] = own[2]

    def wait_path(which):
        for level in range(3):
            size = 2 << level

            @pl.when(lax.rem(y, size) != size // 2)
            def _():
                got = path.at[level, which]
                copy(own.at[0], got, s_dir.at[0, 0], r_dir.at[which, level], mate).wait_recv()

    def permute(table, placed, first, last):
        def move(i, carry):
            base = pl.multiple_of(i * UNROLL, UNROLL)
            for u in range(UNROLL):
                placed[pl.ds(base + u, 1), :] = table[pl.ds(order[0, base + u], 1), :]
            return carry

        lax.fori_loop(first // UNROLL, last // UNROLL, move, 0)

    permute(tv, gv, 0, PTS)

    slot = lax.broadcasted_iota(jnp.int32, (LEAF, R), 0)
    starts = [0]
    for t in range(LEAVES):
        size = sizes[0, t]
        rows[t] = jnp.where(slot < size, gv[pl.ds(starts[t], LEAF), :], 0.0).astype(BF16)
        starts.append(starts[t] + size)
    loads[2].wait()
    for t in range(LEAVES):
        coef[t] = dot(rows[t], basis[t], 0, 0)
    loads[3].wait()
    for j in range(15):
        both = jnp.concatenate([coef[2 * j], coef[2 * j + 1]], axis=1)
        coef[16 + j] = mm(both, transfer[j])
    c_coef().start()

    @pl.when(is0)
    def _():
        @pl.when(y > 0)
        def _():
            m1(1, 0).wait_recv()

        for m in FAR_FIRST:
            mw(m).start()
        wpiece[z] = piece[z, 1]

        @pl.when(y > 0)
        def _():
            m1(1, 1).wait_recv()

        @pl.when(z == 0)
        def _():
            for m in (2, 3, 1):
                m3(m).start()
            xpiece[x] = piece[0]

        for m in FAR_FIRST:
            m2(m).start()

    loads[4].wait()
    for j in range(15):
        term[2 * j] = mmt(coef[2 * j + 1], coupling[j])
        term[2 * j + 1] = mm(coef[2 * j], coupling[j])

    @pl.when(is0)
    def _():
        wait_path(0)
        for level in range(3):
            mat_w[level] = path[level, 0].astype(BF16)
        c_mats().wait_recv()
        c_coef().wait()
        pair = jnp.concatenate([core_mats[0], core_mats[1]], axis=0).astype(BF16)
        prod[0] = mm(jnp.concatenate([coef[30], core_coef[...]], axis=1), pair)
        for level in range(3):
            prod[level + 1] = mm(prod[level], mat_w[level])
        for m in FAR_FIRST:
            ys(m).start()
        for lev in range(3):

            @pl.when(lax.rem(y, 2 << lev) == 1 << lev)
            def _():
                for c in direct_all(lev, 1):
                    c.start()

        yslice[0] = prod[3, pl.ds(pl.multiple_of(16 * y, 16), 16), :]

    @pl.when(is1)
    def _():
        c_coef().wait()

    loads[1].wait()
    for c in range(PTS // 128):
        span = slice(128 * c, 128 * (c + 1))
        tp[span, :] = point_pieces(p_in[:, span]).T
    @pl.when(jnp.logical_and(is0, z == 0))
    def _():
        for m in range(1, 4):
            m3_from(m).wait_recv()
        owner = lax.div(x, 2) * 2 + 1
        xpath[0] = xpiece[owner, 2]
        xpath[1] = xpiece[2, 2]
        xpath[2] = xpiece[owner, lax.rem(x, 2)]
        for m in FAR_FIRST:
            mx(m).start()

    @pl.when(is0)
    def _():
        for m in range(1, 8):
            mw_from(m).wait_recv()
        for i in range(3):
            wlev[y, i] = wpiece[lax.div(z, 2 << i) * (2 << i) + (1 << i)]
        for m in FAR_FIRST:
            m4w(m).start()

    permute(tp, gp, 0, PTS // 2)

    permute(tp, gp, PTS // 2, PTS)

    for t in range(LEAVES):
        pts[t] = gp[pl.ds(starts[t], LEAF), :].astype(BF16)

    eye = (
        lax.broadcasted_iota(jnp.int32, (LEAF, LEAF), 0) == lax.broadcasted_iota(jnp.int32, (LEAF, LEAF), 1)
    ).astype(F32)
    shift = (
        lax.broadcasted_iota(jnp.int32, (R, R), 0) == lax.broadcasted_iota(jnp.int32, (R, R), 1) + 64
    ).astype(F32).astype(BF16)

    def nearby(t, carry):
        left = pts[t]
        right = dot(left, shift).astype(BF16)
        kernel = (jnp.exp(dot(left, right, 1, 1)) + eye).astype(BF16)
        near[t] = dot(kernel, rows[t])
        return carry

    lax.fori_loop(0, 4, nearby, 0, unroll=4)

    @pl.when(is0)
    def _():
        @pl.when(z > 0)
        def _():
            mx(1).wait_recv()

        w8lev[y] = xpath[2]
        for m in FAR_FIRST:
            m6(m).start()
        for m in range(1, 8):
            m2_from(m).wait_recv()
        for i in range(3):
            xlev[y, i] = piece[lax.div(z, 2 << i) * (2 << i) + (1 << i), 2]
        xlev[y, 3:5] = xpath[0:2]
        for m in FAR_FIRST:
            m5(m).start()

    @pl.when(is0)
    def _():
        for m in range(1, 8):
            m4w_from(m).wait_recv()
        for i in range(3):
            mat_w[3 + i] = wlev[:, i].reshape(R, R).astype(BF16)
        for m in range(1, 8):
            ys(m).wait_recv()
        u = yslice[0]
        for m in range(1, 8):
            u = u + yslice[m]
        for i in range(3):
            zsend[i, 0] = u
            u = mm(u, mat_w[3 + i])
        for i in range(3):
            zsend[i, 1] = u
        for m in FAR_FIRST:
            zs(m).start()
        for m in FAR_FIRST:
            yb(m).start()

    lax.fori_loop(4, LEAVES, nearby, 0, unroll=4)

    @pl.when(is0)
    def _():
        for m in range(1, 8):
            m6_from(m).wait_recv()
        mat_w[6] = w8lev[...].reshape(R, R).astype(BF16)

        for m in range(1, 8):
            zs(m).wait_recv()
        u = zsend[0, 1]
        for m in range(1, 8):
            u = u + zgot[m, 1]
        xsend[0] = u
        xsend[1] = mm(u, mat_w[6])
        for m in (2, 3, 1):
            xs(m).start()
        for m in range(1, 8):
            m5_from(m).wait_recv()
        sides = [lax.rem(lax.div(z, 1 << i), 2) for i in range(3)] + [lax.rem(x, 2), lax.div(x, 2)]
        for i in range(5):
            c = xlev[:, i].reshape(R, R)
            mat_c[3 + i] = jnp.where(sides[i] == 0, c.T, c).astype(BF16)
        side_z = [
            mm(zgot[1, 0], mat_c[3]),
            mm(zgot[2, 0] + zgot[3, 0], mat_c[4]),
            mm((zgot[4, 0] + zgot[5, 0]) + (zgot[6, 0] + zgot[7, 0]), mat_c[5]),
        ]
        z_path = mm(dot(mat_w[3], mat_w[4]), mat_w[5])
        x_path = mm(z_path, mat_w[6])
        far[0:R] = exact_mmt(mat_c[7], x_path)
        far[R:] = exact_mmt(mat_c[6], z_path)
        before = mmt(mmt(side_z[2], mat_w[4]) + side_z[1], mat_w[3]) + side_z[0]
        for m in range(1, 4):
            xs(m).wait_recv()
        g = mm3(jnp.concatenate([xgot[2] + xgot[3], xgot[1]], axis=1), far[...]) + before
        gdown[...] = g
        for m in FAR_FIRST:
            yd(m).start()
        fdown[y] = g

        wait_path(1)
        for level in range(3):
            c = path[level, 1]
            mat_c[level] = jnp.where(lax.rem(lax.div(y, 1 << level), 2) == 0, c.T, c).astype(BF16)
        for m in range(1, 8):
            yb(m).wait_recv()
        side_y = [
            mm(yblock[1], mat_c[0]),
            mm(yblock[2] + yblock[3], mat_c[1]),
            mm((yblock[4] + yblock[5]) + (yblock[6] + yblock[7]), mat_c[2]),
        ]
        pair = jnp.concatenate([core_mats[0], core_mats[1]], axis=0).astype(BF16)
        between = core_mats[2].astype(BF16)
        y_path = mm(dot(mat_w[0], mat_w[1]), mat_w[2])
        far[...] = exact_mm(pair, y_path)
        before = mmt(mmt(mmt(side_y[2], mat_w[1]) + side_y[1], mat_w[0]) + side_y[0], pair)
        first = before[:, :R] + mmt(core_coef[...], between)
        second = before[:, R:] + mm(coef[30], between)
        for m in range(1, 8):
            yd_from(m).wait_recv()
        both = mmt3(fdown[...].reshape(R, R), far[...])
        up_field[...] = both[:, R:] + second
        field[30] = both[:, :R] + first
        c_field().start()

    @pl.when(is1)
    def _():
        c_field().wait_recv()

    for j in range(14, -1, -1):
        both = mmt(field[16 + j], transfer[j])
        field[2 * j] = both[:, :R] + term[2 * j]
        field[2 * j + 1] = both[:, R:] + term[2 * j + 1]

    saves = []
    for t in range(LEAVES):
        total[t] = (near[t] + dot(basis[t], field[t].astype(BF16), 1, 1)).astype(BF16)
        if t % 4 == 3:
            saves.append(
                pltpu.make_async_copy(total.at[t - 3 : t + 1], total_any.at[t - 3 : t + 1], s_total.at[t // 4])
            )
            saves[-1].start()
    for save in saves:
        save.wait()

    @pl.when(is1)
    def _():
        c_mats().wait_send()

    @pl.when(is0)
    def _():
        c_field().wait_send()

        @pl.when(y == 0)
        def _():
            for k in range(1, 8):
                m1(k, 0).wait_send()
                m1(k, 1).wait_send()

        for level in range(3):
            size = 2 << level

            @pl.when(lax.rem(y, size) == size // 2)
            def _():
                for c in direct_all(level, 0) + direct_all(level, 1):
                    c.wait_send()

        for m in range(1, 8):
            for group in (mw, m4w, m2, m5, m6, ys, yb, zs, yd):
                group(m).wait_send()
        for m in range(1, 4):
            xs(m).wait_send()

        @pl.when(z == 0)
        def _():
            for m in range(1, 4):
                m3(m).wait_send()
            for m in range(1, 8):
                mx(m).wait_send()


def tree(order, sizes, values, points, basis, transfer, coupling, ctrans, ccoup):
    dma = pltpu.SemaphoreType.DMA
    block = (R, R)
    return pl.pallas_call(
        tree_kernel,
        out_shape=jax.ShapeDtypeStruct((LEAVES, LEAF, R), BF16),
        in_specs=[SMEM, SMEM, HBM, HBM, HBM, HBM, HBM, VMEM, VMEM],
        out_specs=HBM,
        scratch_shapes=[
            pltpu.VMEM((LEAVES, LEAF, R), BF16),
            dma((4,)),
            pltpu.VMEM((PTS, R), BF16),
            pltpu.VMEM((8, PTS), F32),
            pltpu.VMEM((LEAVES, LEAF, R), BF16),
            pltpu.VMEM((LEAVES - 1, 2 * R, R), BF16),
            pltpu.VMEM((LEAVES - 1,) + block, BF16),
            dma((5,)),
            pltpu.VMEM((PTS, R), F32),
            pltpu.VMEM((PTS, R), F32),
            pltpu.VMEM((PTS + LEAF, R), F32),
            pltpu.VMEM((PTS + LEAF, R), F32),
            pltpu.VMEM((LEAVES, LEAF, R), BF16),
            pltpu.VMEM((LEAVES, LEAF, R), BF16),
            pltpu.VMEM((31,) + block, F32),
            pltpu.VMEM((30,) + block, F32),
            pltpu.VMEM((31,) + block, F32),
            pltpu.VMEM((LEAVES, LEAF, R), F32),
            pltpu.VMEM((3,) + block, F32),
            pltpu.VMEM((3,) + block, F32),
            pltpu.VMEM(block, F32),
            pltpu.VMEM(block, F32),
            pltpu.VMEM((3, 2) + block, F32),
            pltpu.VMEM((8, 3, 16, R), F32),
            pltpu.VMEM((8, 16, R), F32),
            pltpu.VMEM((8, 3, 16, R), F32),
            pltpu.VMEM((4, 3, 16, R), F32),
            pltpu.VMEM((3, 16, R), F32),
            pltpu.VMEM((8, 16, R), F32),
            pltpu.VMEM((8, 5, 16, R), F32),
            pltpu.VMEM((7,) + block, BF16),
            pltpu.VMEM((8,) + block, BF16),
            pltpu.VMEM((2 * R, R), F32),
            pltpu.VMEM((4,) + block, F32),
            pltpu.VMEM((8, 16, R), F32),
            pltpu.VMEM((8,) + block, F32),
            pltpu.VMEM((3, 2, 16, R), F32),
            pltpu.VMEM((8, 2, 16, R), F32),
            pltpu.VMEM((2, 16, R), F32),
            pltpu.VMEM((4, 16, R), F32),
            pltpu.VMEM((16, R), F32),
            pltpu.VMEM((8, 16, R), F32),
            dma((3,)), dma((3,)),
            dma((2, 8)), dma((2, 3)),
            dma((2, 8)), dma((2,)),
            dma((8,)), dma((8,)),
            dma((8,)), dma((8,)),
            dma((8,)), dma((8,)),
            dma((4,)), dma((4,)),
            dma((8,)), dma,
            dma((8,)), dma((8,)),
            dma((8,)), dma((8,)),
            dma((8,)), dma((8,)),
            dma((8,)), dma((8,)),
            dma((8,)), dma((8,)),
            dma((4,)), dma((4,)),
            dma((8,)), dma((8,)),
        ],
        compiler_params=pltpu.CompilerParams(
            collective_id=0, has_side_effects=True, vmem_limit_bytes=VMEM_LIMIT
        ),
        name="tree",
    )(order, sizes, values, points, basis, transfer, coupling, ctrans, ccoup)


def body(
    values,
    points,
    tree_order,
    leaf_sizes,
    leaf_basis,
    local_transfer,
    local_coupling,
    cross_transfer,
    cross_coupling,
):
    transfer = local_transfer.reshape(LEAVES - 1, 2 * R, R)
    total = tree(
        tree_order, leaf_sizes, values, points,
        leaf_basis, transfer, local_coupling, cross_transfer, cross_coupling,
    )
    return scatter(total, tree_order, leaf_sizes)


def solution(mesh):
    in_specs = (
        P("leaf", None),
        P(None, "leaf"),
        P("leaf", None),
        P("leaf", None),
        P("leaf", None, None),
        P("leaf", None, None, None),
        P("leaf", None, None),
        P("leaf", None, None, None),
        P("leaf", None, None),
    )
    out_specs = P("leaf", None)
    return jax.shard_map(body, mesh=mesh, in_specs=in_specs, out_specs=out_specs, check_vma=False)
```
